256 devices in a mesh: batch: 64 (over z, x, core), row: 2 (over y_lo), col: 2 (over y_hi).
Axes of the slice: x: 4, y: 4 (y_hi: 2, y_lo: 2; y = y_hi * 2 + y_lo), z: 8, core: 2. Of those that a mesh axis runs over, the one named last changes fastest.
Arguments:
- basis_values: bfloat16 [256, 192, 2048], P(('batch', 'row', 'col')), may hold values from -6 to 6
- density_matrix: bfloat16 [256, 3, 192, 192], P(('batch', 'row', 'col')), may hold values from -0.03125 to 0.03125
- points: float32 [256, 3, 2048], P(('batch', 'row', 'col')), may hold values from -2 to 2
- weights: float32 [256, 2048], P(('batch', 'row', 'col')), may hold values from 0.128 to 1.28
- intersection: int32 [256, 32], P(('batch', 'row', 'col')), may hold values from 0 to 255, as said below
- basis_index: int32 [256, 192], P(('batch', 'row', 'col')), may hold values from 0 to 1535, as said below
- atom_positions: float32 [3, 256], replicated, may hold values from -2 to 2
- shell_blocks: int32 [256], replicated, may hold values from 1 to 8
- shell_widths: float32 [64], replicated, may hold values from 0.03125 to 0.0625
- green: bfloat16 [256, 8, 4096], P('batch'), may hold values from -0.0009765625 to 0.0009765625
Outputs:
- potential: bfloat16 [256, 12288], P('batch')
- hamiltonian: bfloat16 [3, 1536, 1536], P(None, 'row', 'col')
The draws below stay inside these ranges and needn't reach their ends.
Inputs may be any that keep to these rules, and one draw needn't show every extreme that they name: `intersection`: within a batch the 32 atom numbers are distinct. The owner of atom a is a // 4; no owner holds more than 1 of one batch's atoms, and among the batches with equal row and col index one owner holds exactly 1 of the atoms of every such batch. `basis_index`: within a batch the numbers are distinct, and its q-th run of 96 entries lies in [q * 768, (q + 1) * 768).
All inputs are finite; a program needn't handle non-finite values.
Results may differ from the reference program's by a relative error of at most 0.0095.
Values may be sent and summed in bfloat16 or wider, within the bound.
A program may use at most 128 MiB of HBM per device.

```python
import math
import jax
import jax.numpy as jnp
from jax import lax

NBF = 192
P_SIZE = 2048
S = 64
DEG = 8
K_OV = 32
A_DEV = 4
NB = 1536
L = 64
SHB = 8
BATCHES = 256
ATOMS = 256
N_BATCH = 64
N_ROW = 2
N_COL = 2


def draw_intersection(key, part):
    batches = N_BATCH * N_ROW * N_COL
    planes = N_ROW * N_COL
    cap = (K_OV + N_BATCH - 1) // N_BATCH
    pairs = N_BATCH * cap
    base = jax.random.fold_in(key, 11)
    first_key, second_key, third_key = jax.random.split(base, 3)
    star = jax.random.randint(first_key, (planes,), 0, N_BATCH)
    plane_of = jnp.arange(batches) % planes
    star_of = jnp.take(star, plane_of)
    noise = jax.random.randint(second_key, (batches, pairs), 0, 1 << 20)
    pair_ids = jnp.arange(pairs)
    special = pair_ids[None, :] // cap == star_of[:, None]
    score = (noise + jnp.where(special, 1 << 21, 0)) * pairs + pair_ids[None, :]
    chosen = lax.top_k(score, K_OV)[1]
    owner = chosen // cap
    rank = chosen % cap
    orders = jax.vmap(lambda single: jax.random.permutation(single, A_DEV))(jax.random.split(third_key, batches))
    local = jnp.take_along_axis(orders, rank, axis=1)
    return (owner * A_DEV + local).astype(jnp.int32)


def draw_basis_index(key, part):
    batches = N_BATCH * N_ROW * N_COL
    span = NB // N_ROW
    each = NBF // N_ROW
    keys = jax.random.split(jax.random.fold_in(key, 23), batches * N_ROW)
    picks = jax.vmap(lambda single: jax.random.permutation(single, span)[:each])(keys).reshape(batches, N_ROW, each)
    offsets = (jnp.arange(N_ROW) * span)[None, :, None]
    return (picks + offsets).reshape(batches, NBF).astype(jnp.int32)


def place_ends(values, rng, low, high):
    index_at = [jax.random.randint(jax.random.fold_in(rng, axis), (), 0, length) for axis, length in enumerate(values.shape)]
    widest = values.shape.index(max(values.shape))
    neighbour = index_at[:widest] + [(index_at[widest] + 1) % values.shape[widest]] + index_at[widest + 1:]
    return values.at[tuple(index_at)].set(low).at[tuple(neighbour)].set(high)


def level_of(key, extent, cuts, low, largest):
    def one(position, shards_of):
        draws = jax.random.uniform(jax.random.fold_in(jax.random.fold_in(key, 6), position), (shards_of,), jnp.float32, low / len(cuts), largest / len(cuts))
        return jnp.repeat(jnp.exp(draws), extent[position] // shards_of).reshape((-1,) + (1,) * (len(extent) - position - 1))

    gain = one(*cuts[0])
    for cut in cuts[1:]:
        gain = gain * one(*cut)
    return gain


def centred(key, shape, scale, limit, pieces=(), held_as=jnp.bfloat16):
    array = scale * jax.random.normal(key, shape, jnp.float32)
    if pieces:
        array = array * level_of(key, shape, pieces, -0.22, 0.18)
    return jnp.clip(array, -limit, limit).astype(held_as)


def setup_inputs(seed: int = 0) -> dict:
    seeds = jax.random.split(jax.random.key(seed), 11)
    basis_values = centred(seeds[0], (BATCHES, NBF, P_SIZE), 1.0, 6.0, ((0, 256),))
    density_matrix = centred(seeds[1], (BATCHES, 3, NBF, NBF), (1.0 / NBF), 0.03125, ((0, 256),))
    points = jnp.clip(jax.random.uniform(seeds[2], (BATCHES, 3, P_SIZE), jnp.float32, -2.0, 2.0) * level_of(seeds[2], (BATCHES, 3, P_SIZE), ((0, 256),), -0.4, 0.0), -2.0, 2.0)
    weights = jnp.clip(jnp.exp(math.log(1.28) - 2.30258502 * jax.random.uniform(seeds[3], (BATCHES, P_SIZE), jnp.float32) ** level_of(seeds[3], (BATCHES, P_SIZE), ((0, 256),), -0.2, 0.2)), 0.128, 1.28)
    intersection = draw_intersection(jax.random.fold_in(seeds[10], 71), 0)
    basis_index = draw_basis_index(jax.random.fold_in(seeds[10], 71), 0)
    atom_positions = jnp.clip(jax.random.uniform(seeds[6], (3, ATOMS), jnp.float32, -2.0, 2.0), -2.0, 2.0)
    shell_blocks = place_ends(jax.random.randint(seeds[7], (ATOMS,), 1, SHB + 1), jax.random.fold_in(seeds[7], 1), 1, SHB).astype(jnp.int32)
    shell_widths = jnp.clip(jnp.exp(jax.random.uniform(seeds[8], (S,), jnp.float32, math.log(0.03125), math.log(0.0625))), 0.03125, 0.0625)
    green = centred(seeds[9], (ATOMS, DEG, S * S), (4 * S * L * L * K_OV) ** -0.5, 0.0009765625, ((0, 64),))
    return dict(basis_values=basis_values, density_matrix=density_matrix, points=points, weights=weights, intersection=intersection, basis_index=basis_index, atom_positions=atom_positions, shell_blocks=shell_blocks, shell_widths=shell_widths, green=green)


def chebyshev(values, count):
    terms = [jnp.ones_like(values), values]
    for order in range(2, count):
        terms.append(2.0 * values * terms[-1] - terms[-2])
    return jnp.stack(terms[:count], axis=0)

def atom_tables(spots, centre, blocks, shell_widths):
    delta = spots - centre[:, None]
    dist = jnp.sqrt(lax.optimization_barrier(jnp.sum(delta * delta, axis=0)) + 0.01)
    unit = delta / dist[None, :]
    shells = shell_widths.shape[0]
    middle = 4.0 * jnp.arange(shells).astype(jnp.float32) / shells
    live = jnp.arange(shells).astype(jnp.int32) < 8 * blocks
    bump = jnp.exp(-jnp.square((dist[None, :] - middle[:, None]) / shell_widths[:, None]))
    radial = jnp.where(live[:, None], bump, jnp.zeros_like(bump))
    polar = chebyshev(unit[2], DEG)
    side = chebyshev(unit[0], DEG)
    angular = (polar[:, None, :] * side[None, :, :]).reshape(DEG * DEG, spots.shape[1])
    return (radial, angular.astype(jnp.bfloat16))

def batch_tables(spots, atoms, atom_positions, shell_blocks, shell_widths):
    centres = jnp.take(atom_positions, atoms, axis=1).T
    counts = jnp.take(shell_blocks, atoms)
    return jax.vmap(atom_tables, in_axes=(None, 0, 0, None))(spots, centres, counts, shell_widths)

def reference(basis_values, density_matrix, points, weights, intersection, basis_index, atom_positions, shell_blocks, shell_widths, green):
    atoms_total = green.shape[0]
    width = 3 * S * DEG * DEG
    highest = lax.Precision.HIGHEST

    def first_pass(total, item):
        phi, dens, spots, measure, atoms = item
        phi_wide = phi.astype(jnp.float32)
        dphi = jnp.einsum('cij,jp->cip', dens.astype(jnp.float32), phi_wide)
        density = lax.optimization_barrier(jnp.sum(phi_wide[None] * dphi, axis=1))
        radial, angular = batch_tables(spots, atoms, atom_positions, shell_blocks, shell_widths)
        weighted = measure[None, :] * density
        scaled = lax.optimization_barrier((radial[:, None] * weighted[None, :, None, :]).astype(jnp.bfloat16))
        moments = jnp.einsum('kcsp,klp->kcsl', scaled.astype(jnp.float32), angular.astype(jnp.float32))
        return (total.at[atoms].add(moments.reshape(atoms.shape[0], width)), None)
    total, _ = lax.scan(first_pass, jnp.zeros((atoms_total, width), jnp.float32), (basis_values, density_matrix, points, weights, intersection))
    charges = lax.optimization_barrier(total.astype(jnp.bfloat16)).astype(jnp.float32)
    charges = charges.reshape(atoms_total, 3, S, DEG, DEG)
    kernels = green.astype(jnp.float32).reshape(atoms_total, DEG, S, S)
    potential = jnp.einsum('xast,xctam->xcsam', kernels, charges).astype(jnp.bfloat16).reshape(atoms_total, width)

    def second_pass(tiles, item):
        phi, spots, measure, atoms, labels = item
        radial, angular = batch_tables(spots, atoms, atom_positions, shell_blocks, shell_widths)
        tables = jnp.take(potential, atoms, axis=0).astype(jnp.float32).reshape(atoms.shape[0], 3, S, DEG * DEG)
        spread = jnp.einsum('kcsl,klp->kcsp', tables, angular.astype(jnp.float32))
        field = jnp.einsum('ksp,kcsp->cp', radial, spread, precision=highest)
        phi_wide = phi.astype(jnp.float32)
        operand = lax.optimization_barrier((phi_wide[None] * (measure[None, :] * field)[:, None, :]).astype(jnp.bfloat16))
        local = jnp.einsum('cip,jp->cij', operand.astype(jnp.float32), phi_wide)
        local = lax.optimization_barrier(local.astype(jnp.bfloat16)).astype(jnp.float32)
        return (tiles.at[:, labels[:, None], labels[None, :]].add(local), None)
    tiles, _ = lax.scan(second_pass, jnp.zeros((3, NB, NB), jnp.float32), (basis_values, points, weights, intersection, basis_index))
    return (potential, tiles.astype(jnp.bfloat16))
```

```python
import math

import jax
import jax.numpy as jnp
from jax import lax
from jax.experimental import pallas as pl
from jax.experimental.pallas import tpu as pltpu
from jax.sharding import Mesh
from jax.sharding import PartitionSpec as P

S = 64
DEG = 8
L = 64
NB = 1536
BATCH = ("batch_0", "batch_1", "batch_2")
BATCH_ROW_COL = ("batch_0", "batch_1", "batch_2", "row", "col")
MESH = pl.DeviceIdType.MESH
F32 = jnp.float32
BF16 = jnp.bfloat16
HALF_S = S // 2
VMEM_LIMIT = 56 * 1024 * 1024
NT = (((1,), (1,)), ((), ()))


def vmem():
    return pl.BlockSpec(memory_space=pltpu.VMEM)


def smem():
    return pl.BlockSpec(memory_space=pltpu.SMEM)


def fill_rows(atoms_ref, pos_ref, pts_ref, dist_ref, polar_ref, side_ref):
    count = atoms_ref.shape[0]
    every = pos_ref.shape[1]
    picked = lax.broadcasted_iota(jnp.int32, (count, every), 1) == atoms_ref[...]
    centre = [
        jnp.sum(jnp.where(picked, pos_ref[d : d + 1, :], 0.0), axis=1, keepdims=True)
        for d in range(3)
    ]
    for group in range(count // 8):
        rows = slice(group * 8, group * 8 + 8)
        dx, dy, dz = [pts_ref[d : d + 1, :] - centre[d][rows] for d in range(3)]
        dist = jnp.sqrt(dx * dx + dy * dy + dz * dz + 0.01)
        inverse = 1.0 / dist
        dist_ref[group] = dist
        for value, ref in ((dz * inverse, polar_ref), (dx * inverse, side_ref)):
            older, newer = jnp.ones_like(value), value
            ref[0, group] = older
            ref[1, group] = newer
            for order in range(2, DEG):
                older, newer = newer, 2.0 * value * newer - older
                ref[order, group] = newer


def shell_rows(widths_ref, lanes):
    row = lax.broadcasted_iota(jnp.int32, (S, lanes), 0)
    shell = jnp.where(row < HALF_S, 2 * row, 2 * (row - HALF_S) + 1)
    middle = shell.astype(F32) * (4.0 / S)
    scale = math.sqrt(math.log2(math.e)) / widths_ref[...]
    return shell, middle, scale


def radial_of(dist, middle, scale, live):
    t = (dist - middle) * scale
    return jnp.where(live, jnp.exp2(-(t * t)), 0.0)


def angular_of(polar_ref, side_ref, group, u, cols):
    side = jnp.concatenate([side_ref[j, group, u : u + 1, cols] for j in range(DEG)], axis=0)
    return jnp.concatenate(
        [side * polar_ref[i, group, u : u + 1, cols] for i in range(DEG)], axis=0
    ).astype(BF16)


def moments_kernel(
    atoms_s, blocks_s, atoms_ref, pos_ref, pts_ref, w_ref, widths_ref, phi_ref, dens_ref,
    out_ref, dist_ref, polar_ref, side_ref, wd_ref, scaled_ref, ang_ref, mid_ref, inv_ref,
):
    count = atoms_ref.shape[0]
    points = phi_ref.shape[1]
    fill_rows(atoms_ref, pos_ref, pts_ref, dist_ref, polar_ref, side_ref)
    wide = min(512, points)
    for first in range(0, points, wide):
        cols = slice(first, first + wide)
        phi = phi_ref[:, cols]
        for c in range(3):
            dphi = jnp.dot(dens_ref[c], phi, preferred_element_type=F32)
            total = jnp.sum(phi.astype(F32) * dphi, axis=0, keepdims=True)
            wd_ref[c : c + 1, cols] = total * w_ref[:, cols]
    shell, middle, scale = shell_rows(widths_ref, 128)
    mid_ref[...] = middle
    inv_ref[...] = scale
    out_ref[count] = jnp.zeros((3 * HALF_S, 2 * L), BF16)

    def eight(group, carry):
        for u in range(8):
            k = group * 8 + u
            b = u % 2
            live = shell < 8 * blocks_s[atoms_s[0, k]]
            for first in range(0, points, 128):
                cols = slice(first, first + 128)
                rad = radial_of(dist_ref[group, u : u + 1, cols], mid_ref[...], inv_ref[...], live)
                for c in range(3):
                    part = (rad * wd_ref[c : c + 1, cols]).astype(BF16)
                    for par in range(2):
                        row = par * 96 + c * HALF_S
                        scaled_ref[b, row : row + HALF_S, cols] = part[
                            par * HALF_S : (par + 1) * HALF_S
                        ]
                ang_ref[b, :, cols] = angular_of(polar_ref, side_ref, group, u, cols)
            got = lax.dot_general(scaled_ref[b], ang_ref[b], NT, preferred_element_type=F32)
            out_ref[k] = jnp.concatenate([got[:96], got[96:]], axis=1).astype(BF16)
        return carry

    lax.fori_loop(0, count // 8, eight, 0)


def moments_call(atoms, blocks, atoms_col, pos, pts, w, widths, phi, dens):
    count = atoms.shape[1]
    points = phi.shape[1]
    return pl.pallas_call(
        moments_kernel,
        out_shape=jax.ShapeDtypeStruct((count + 1, 96, 128), BF16),
        in_specs=[smem(), smem()] + [vmem()] * 7,
        out_specs=vmem(),
        scratch_shapes=[
            pltpu.VMEM((count // 8, 8, points), F32),
            pltpu.VMEM((DEG, count // 8, 8, points), F32),
            pltpu.VMEM((DEG, count // 8, 8, points), F32),
            pltpu.VMEM((8, points), F32),
            pltpu.VMEM((2, 192, points), BF16),
            pltpu.VMEM((2, L, points), BF16),
            pltpu.VMEM((S, 128), F32),
            pltpu.VMEM((S, 128), F32),
        ],
        compiler_params=pltpu.CompilerParams(vmem_limit_bytes=VMEM_LIMIT),
        cost_estimate=pl.CostEstimate(flops=4_000_000_000, bytes_accessed=3_000_000, transcendentals=4_000_000),
        name="moments",
    )(atoms, blocks, atoms_col, pos, pts, w, widths, phi, dens)


class Rings:
    def __init__(self, send, recv):
        self.send, self.recv = send, recv
        self.used = 0
        self.started = []
        self.core = lax.axis_index("batch_2")
        self.turn = 1 - 2 * self.core
        rows = lax.axis_size("row")
        self.size = {
            "z": lax.axis_size("batch_0"),
            "x": lax.axis_size("batch_1"),
            "y": rows * lax.axis_size("col"),
        }
        self.at = {
            "z": lax.axis_index("batch_0"),
            "x": lax.axis_index("batch_1"),
            "y": lax.axis_index("col") * rows + lax.axis_index("row"),
        }

    def place(self, axis, shift):
        n = self.size[axis]
        return lax.rem(self.at[axis] + shift + 2 * n, n)

    def device(self, axis, shift):
        spot = self.place(axis, shift)
        if axis == "z":
            return {"batch_0": spot}
        if axis == "x":
            return {"batch_1": spot}
        rows = lax.axis_size("row")
        return {"row": lax.rem(spot, rows), "col": spot // rows}

    def sibling(self):
        return {"batch_2": 1 - self.core}

    def greet(self, axes, others=()):
        barrier = pltpu.get_barrier_semaphore()
        greeted = 0
        for axis in axes:
            if self.size[axis] > 1:
                for shift in (1, -1):
                    pl.semaphore_signal(
                        barrier, inc=1, device_id=self.device(axis, shift), device_id_type=MESH
                    )
                    greeted += 1
        for other in others:
            pl.semaphore_signal(barrier, inc=1, device_id=other, device_id_type=MESH)
            greeted += 1
        pl.semaphore_wait(barrier, greeted)

    def ticket(self):
        self.used += 1
        return self.used - 1

    def copy(self, src, dst, ticket, device):
        made = pltpu.make_async_remote_copy(
            src_ref=src, dst_ref=dst, send_sem=self.send.at[ticket],
            recv_sem=self.recv.at[ticket], device_id=device, device_id_type=MESH,
        )
        made.start()
        self.started.append(made)

    def arrive(self, dst, ticket):
        pltpu.make_async_remote_copy(
            src_ref=dst, dst_ref=dst, send_sem=self.send.at[ticket],
            recv_sem=self.recv.at[ticket], device_id=self.sibling(), device_id_type=MESH,
        ).wait_recv()

    def finish(self):
        for made in self.started:
            made.wait_send()

    def reduce(self, buf, base, rows, axis, slots, spot):
        n = self.size[axis]
        if n == 1:
            return
        here = self.at[axis]
        lanes = [(1, n // 2), (-1, n // 2 - 1)]
        tickets = [[self.ticket() for _ in range(steps)] for _, steps in lanes]
        places = []
        for _, steps in lanes:
            places.append([spot + rows * k for k in range(steps)])
            spot += rows * steps

        def own(shift):
            return pl.ds(pl.multiple_of(base + self.place(axis, shift) * rows, 16), rows)

        for t in range(n // 2):
            for lane, (way, steps) in enumerate(lanes):
                if t >= steps:
                    continue
                mine = own(-way * self.turn * (steps - t))
                if t == 0:
                    source = buf.at[mine]
                else:
                    source = slots.at[pl.ds(places[lane][t - 1], rows)]
                    yield
                    self.arrive(source, tickets[lane][t - 1])
                    source[...] = (source[...].astype(F32) + buf[mine, :].astype(F32)).astype(BF16)
                self.copy(
                    source, slots.at[pl.ds(places[lane][t], rows)], tickets[lane][t],
                    self.device(axis, -way * self.turn),
                )
        total = buf[own(0), :].astype(F32)
        for lane, (way, steps) in enumerate(lanes):
            if steps:
                source = slots.at[pl.ds(places[lane][-1], rows)]
                yield
                self.arrive(source, tickets[lane][-1])
                total = total + source[...].astype(F32)
        buf[own(0), :] = total.astype(BF16)

    def gather(self, buf, base, rows, axis, arrived=None):
        n = self.size[axis]
        if arrived:
            arrived(0)
        if n == 1:
            return
        lanes = [(1, n // 2), (-1, n // 2 - 1)]
        tickets = [[self.ticket() for _ in range(steps)] for _, steps in lanes]

        def chunk(shift):
            start = pl.multiple_of(base + self.place(axis, shift) * rows, 16)
            return buf.at[pl.ds(start, rows)]

        for t in range(n // 2 + 1):
            for lane, (way, steps) in enumerate(lanes):
                if t > steps or steps == 0:
                    continue
                block = chunk(way * self.turn * t)
                if t > 0:
                    yield
                    self.arrive(block, tickets[lane][t - 1])
                if t < steps:
                    self.copy(block, block, tickets[lane][t], self.device(axis, -way * self.turn))
                if t > 0 and arrived:
                    arrived(way * t)


def run_together(tasks):
    tasks = list(tasks)
    while tasks:
        for task in list(tasks):
            try:
                next(task)
            except StopIteration:
                tasks.remove(task)


def spread_out(rings, tab, base, total_rows, axes, forwards):
    mine = tab.at[rings.core]
    levels = []
    rows, start = total_rows, base
    for axis in axes:
        rows //= rings.size[axis]
        levels.append((axis, start, rows))
        start = start + rings.at[axis] * rows
    for depth in reversed(range(len(levels))):
        axis, first, rows = levels[depth]

        def forward(shift, axis=axis, first=first, rows=rows):
            ticket = rings.ticket()
            signed = shift * rings.turn
            here = pl.ds(pl.multiple_of(first + rings.place(axis, signed) * rows, 16), rows)
            there = pl.ds(pl.multiple_of(first + rings.place(axis, -signed) * rows, 16), rows)
            rings.copy(tab.at[rings.core, here], tab.at[rings.core, here], ticket, rings.sibling())
            forwards.append((tab.at[1 - rings.core, there], ticket))

        yield from rings.gather(mine, first, rows, axis, forward if depth == 0 else None)


def collect(rings, buf, base, total_rows, axes, slots, spot):
    rows, start = total_rows, base
    for axis in axes:
        rows //= rings.size[axis]
        yield from rings.reduce(buf, start, rows, axis, slots, spot)
        spot += rows * (rings.size[axis] - 1)
        start = start + rings.at[axis] * rows


def chunk_start(rings, base, total_rows, axes):
    rows, start = total_rows, base
    for axis in axes:
        rows //= rings.size[axis]
        start = start + rings.at[axis] * rows
    return start, rows


ATOM_ORDERS = (("y", "x", "z"), ("z", "y", "x"), ("x", "z", "y"))


def atoms_kernel(
    own_s, sib_s, mom_ref, green_ref, tab_ref, pot_ref, dense, slots, other, send, recv
):
    rings = Rings(send, recv)
    nz, nx, ny = (rings.size[a] for a in "zxy")
    held = nz * nx * ny
    part_rows = held * HALF_S
    rings.greet("zxy", [rings.sibling()])
    ticket = rings.ticket()
    rings.copy(mom_ref, other, ticket, rings.sibling())
    rings.arrive(other, ticket)

    def place(slot, order):
        spots = {"z": slot // (nx * ny), "x": lax.rem(slot // ny, nx), "y": lax.rem(slot, ny)}
        index = 0
        for axis in order:
            index = index * rings.size[axis] + spots[axis]
        return index

    def fill(slot, carry):
        value = mom_ref[own_s[0, slot]] + other[sib_s[0, slot]]
        for part, order in enumerate(ATOM_ORDERS):
            row = pl.multiple_of(part * part_rows + place(slot, order) * HALF_S, 32)
            dense[pl.ds(row, HALF_S), :] = value[part * HALF_S : (part + 1) * HALF_S]
        return carry

    lax.fori_loop(0, held, fill, 0)
    forwards = []
    green = green_ref[...]
    column = lax.broadcasted_iota(jnp.int32, (DEG, HALF_S, L), 2) // DEG
    layer = lax.broadcasted_iota(jnp.int32, (DEG, HALF_S, L), 0)

    def task(part):
        order = ATOM_ORDERS[part]
        base = part * part_rows
        yield from collect(rings, dense, base, part_rows, order, slots, base)
        start, rows = chunk_start(rings, base, part_rows, order)
        here = pl.ds(pl.multiple_of(start, 32), rows)
        charges = dense[here, :].astype(F32)
        stacked = jnp.concatenate([charges[:, :L], charges[:, L:]], axis=0).astype(BF16)
        result = jnp.dot(green, stacked, preferred_element_type=F32)
        sides = []
        for par in range(2):
            block = result[par * DEG * HALF_S : (par + 1) * DEG * HALF_S].reshape(DEG, HALF_S, L)
            sides.append(jnp.sum(jnp.where(column == layer, block, 0.0), axis=0))
        tab_ref[rings.core, here, :] = jnp.concatenate(sides, axis=1).astype(BF16)
        yield from spread_out(rings, tab_ref, base, part_rows, order, forwards)

    run_together(task(part) for part in range(3))
    for slot in range(ny):
        for part, order in enumerate(ATOM_ORDERS):
            index = 0
            for axis in order:
                index = index * rings.size[axis] + (slot if axis == "y" else rings.at[axis])
            row = pl.multiple_of(part * part_rows + index * HALF_S, 32)
            pot_ref[slot, part * HALF_S : (part + 1) * HALF_S, :] = tab_ref[
                rings.core, pl.ds(row, HALF_S), :
            ]
    for block, ticket in forwards:
        rings.arrive(block, ticket)
    rings.finish()


def atoms_call(own, sib, moments, green, planes):
    held = own.shape[1]
    return pl.pallas_call(
        atoms_kernel,
        out_shape=(
            jax.ShapeDtypeStruct((2, 3 * held * HALF_S, 128), BF16),
            jax.ShapeDtypeStruct((planes, 96, 128), BF16),
        ),
        in_specs=[smem(), smem(), vmem(), vmem()],
        out_specs=(vmem(), vmem()),
        scratch_shapes=[
            pltpu.VMEM((3 * held * HALF_S, 128), BF16),
            pltpu.VMEM((3 * held * HALF_S, 128), BF16),
            pltpu.VMEM(moments.shape, BF16),
            pltpu.SemaphoreType.DMA((112,)),
            pltpu.SemaphoreType.DMA((112,)),
        ],
        compiler_params=pltpu.CompilerParams(
            vmem_limit_bytes=VMEM_LIMIT, collective_id=0, has_side_effects=True
        ),
        cost_estimate=pl.CostEstimate(flops=100_000_000, bytes_accessed=60_000_000, transcendentals=0),
        name="atoms",
    )(own, sib, moments, green)


def field_kernel(
    rows_s, atoms_s, blocks_s, atoms_ref, pos_ref, pts_ref, w_ref, widths_ref, phi_ref, tab_ref,
    out_ref, dist_ref, polar_ref, side_ref, acc_ref, operand_ref, pad_ref, mid_ref, inv_ref,
):
    count = atoms_ref.shape[0]
    points = phi_ref.shape[1]
    basis = phi_ref.shape[0]
    piece = basis // 2
    fill_rows(atoms_ref, pos_ref, pts_ref, dist_ref, polar_ref, side_ref)
    wide = min(256, points)
    shell, middle, scale = shell_rows(widths_ref, wide)
    mid_ref[...] = middle
    inv_ref[...] = scale
    acc_ref[...] = jnp.zeros_like(acc_ref)

    def eight(group, carry):
        for u in range(8):
            k = group * 8 + u
            live = shell < 8 * blocks_s[atoms_s[0, k]]
            packed = [
                tab_ref[pl.ds(pl.multiple_of(rows_s[c, k], 32), HALF_S), :] for c in range(3)
            ]
            packed = jnp.concatenate(packed, axis=0)
            table = jnp.concatenate([packed[:, :L], packed[:, L:]], axis=0)
            for first in range(0, points, wide):
                cols = slice(first, first + wide)
                ang = angular_of(polar_ref, side_ref, group, u, cols)
                spread = jnp.dot(table, ang, preferred_element_type=F32)
                rad = radial_of(dist_ref[group, u : u + 1, cols], mid_ref[...], inv_ref[...], live)
                for c in range(3):
                    total = acc_ref[c, :, cols]
                    for par in range(2):
                        row = par * 96 + c * HALF_S
                        prod = spread[row : row + HALF_S] * rad[par * HALF_S : (par + 1) * HALF_S]
                        for g in range(0, HALF_S, 8):
                            total = total + prod[g : g + 8]
                    acc_ref[c, :, cols] = total
        return carry

    lax.fori_loop(0, count // 8, eight, 0)
    for q in range(2):
        pad_ref[q, :piece, :] = phi_ref[q * piece : (q + 1) * piece, :]
        pad_ref[q, piece:, :] = jnp.zeros((128 - piece, points), BF16)
    for c in range(3):
        field = jnp.sum(acc_ref[c], axis=0, keepdims=True) * w_ref[...]
        for first in range(0, points, wide):
            cols = slice(first, first + wide)
            operand_ref[:, cols] = (phi_ref[:, cols].astype(F32) * field[:, cols]).astype(BF16)
        for q in range(2):
            local = lax.dot_general(
                operand_ref[...], pad_ref[q], NT, preferred_element_type=F32
            ).astype(BF16)
            for r in range(2):
                out_ref[r * 2 + q, :, c * 128 : (c + 1) * 128] = local[r * piece : (r + 1) * piece]


def field_call(rows, atoms, blocks, atoms_col, pos, pts, w, widths, phi, tab):
    count = atoms.shape[1]
    basis, points = phi.shape
    wide = min(256, points)
    return pl.pallas_call(
        field_kernel,
        out_shape=jax.ShapeDtypeStruct((4, basis // 2, 384), BF16),
        in_specs=[smem()] * 3 + [vmem()] * 7,
        out_specs=vmem(),
        scratch_shapes=[
            pltpu.VMEM((count // 8, 8, points), F32),
            pltpu.VMEM((DEG, count // 8, 8, points), F32),
            pltpu.VMEM((DEG, count // 8, 8, points), F32),
            pltpu.VMEM((3, 8, points), F32),
            pltpu.VMEM((basis, points), BF16),
            pltpu.VMEM((2, 128, points), BF16),
            pltpu.VMEM((S, wide), F32),
            pltpu.VMEM((S, wide), F32),
        ],
        compiler_params=pltpu.CompilerParams(vmem_limit_bytes=VMEM_LIMIT),
        cost_estimate=pl.CostEstimate(flops=4_000_000_000, bytes_accessed=8_000_000, transcendentals=4_000_000),
        name="field",
    )(rows, atoms, blocks, atoms_col, pos, pts, w, jnp.broadcast_to(widths[:, :1], (S, wide)), phi, tab)


TILE_ORDERS = (("z", "x"), ("x", "z"))


def matrix_kernel(quads_ref, label_ref, tab_ref, flat, slots, got, marks, placed, hit, send, recv):
    rings = Rings(send, recv)
    row, col, core = (lax.axis_index(a) for a in ("row", "col", "batch_2"))
    n_row, n_col = lax.axis_size("row"), lax.axis_size("col")
    piece = quads_ref.shape[1]
    tile = hit.shape[0]
    half = tile // 2
    me = (core * n_row + row) * n_col + col
    shifts = [
        (dc, dr, dl) for dc in range(2) for dr in range(n_row) for dl in range(n_col)
    ][1:]

    def peer(shift):
        return {
            "batch_2": lax.rem(core + shift[0], 2),
            "row": lax.rem(row + shift[1], n_row),
            "col": lax.rem(col + shift[2], n_col),
        }

    rings.greet("zx", [peer(shift) for shift in shifts])
    waits = []
    for shift in shifts:
        to = peer(shift)
        first, second = rings.ticket(), rings.ticket()
        rings.copy(label_ref, marks.at[me], first, to)
        rings.copy(quads_ref.at[to["row"] * 2 + to["col"]], got.at[me], second, to)
        source = (to["batch_2"] * n_row + to["row"]) * n_col + to["col"]
        waits.append((marks.at[source], first, got.at[source], second))
    marks[me] = label_ref[...]
    got[me] = quads_ref[row * 2 + col]
    padded = flat.shape[0] - 3 * half * (tile // 128)
    flat[flat.shape[0] - padded :, :] = jnp.zeros((padded, 128), BF16)
    for mark, first, block, second in waits:
        rings.arrive(mark, first)
        rings.arrive(block, second)
    sources = 2 * n_row * n_col
    for s in range(sources):
        label = marks[s]
        rows_at = jnp.where(row == 0, label[0:1, :], label[1:2, :]) - row * tile - core * half
        cols_at = jnp.where(col == 0, label[0:1, :], label[1:2, :]) - col * tile
        row_hit = lax.broadcasted_iota(jnp.int32, (half, 128), 0) == rows_at
        row_hit = jnp.where(row_hit, 1.0, 0.0).astype(BF16)[:, :piece]
        spread = jnp.dot(row_hit, got[s], preferred_element_type=F32).astype(BF16)
        for c in range(3):
            placed[c * half : (c + 1) * half, s * 128 : (s + 1) * 128] = spread[
                :, c * 128 : (c + 1) * 128
            ]
        col_hit = lax.broadcasted_iota(jnp.int32, (tile, 128), 0) == cols_at
        hit[:, s * 128 : (s + 1) * 128] = jnp.where(col_hit, 1.0, 0.0).astype(BF16)
    groups = tile // 128
    for c in range(3):
        for j in range(tile // 256):
            block = lax.dot_general(
                placed[c * half : (c + 1) * half, :], hit[j * 256 : (j + 1) * 256, :], NT,
                preferred_element_type=F32,
            ).astype(BF16)
            for h in range(2):
                start = (c * groups + 2 * j + h) * half
                flat[start : start + half, :] = block[:, h * 128 : (h + 1) * 128]
    part_rows = flat.shape[0] // 2
    forwards = []

    def task(part):
        order = TILE_ORDERS[part]
        base = part * part_rows
        yield from collect(rings, flat, base, part_rows, order, slots, base)
        start, rows = chunk_start(rings, base, part_rows, order)
        here = pl.ds(pl.multiple_of(start, 16), rows)
        tab_ref[rings.core, here, :] = flat[here, :]
        yield from spread_out(rings, tab_ref, base, part_rows, order, forwards)

    run_together(task(part) for part in range(2))
    for block, ticket in forwards:
        rings.arrive(block, ticket)
    rings.finish()


def matrix_call(quads, labels, tile, ring_devices):
    half = tile // 2
    used = 3 * half * (tile // 128)
    unit = 2 * 16 * ring_devices
    rows = -(-used // unit) * unit
    sources = 8
    piece = quads.shape[1]
    return pl.pallas_call(
        matrix_kernel,
        out_shape=jax.ShapeDtypeStruct((2, rows, 128), BF16),
        in_specs=[vmem(), vmem()],
        out_specs=vmem(),
        scratch_shapes=[
            pltpu.VMEM((rows, 128), BF16),
            pltpu.VMEM((rows, 128), BF16),
            pltpu.VMEM((sources, piece, 384), BF16),
            pltpu.VMEM((sources, 8, 128), jnp.int32),
            pltpu.VMEM((3 * half, sources * 128), BF16),
            pltpu.VMEM((tile, sources * 128), BF16),
            pltpu.SemaphoreType.DMA((80,)),
            pltpu.SemaphoreType.DMA((80,)),
        ],
        compiler_params=pltpu.CompilerParams(
            vmem_limit_bytes=VMEM_LIMIT, collective_id=1, has_side_effects=True
        ),
        cost_estimate=pl.CostEstimate(flops=2_000_000_000, bytes_accessed=60_000_000, transcendentals=0),
        name="matrix",
    )(quads, labels)


def layout_kernel(tab_ref, out_ref):
    tile = out_ref.shape[2]
    half = tile // 2
    for h in range(2):
        for g in range(tile // 128):
            out_ref[0, h * half : (h + 1) * half, g * 128 : (g + 1) * 128] = tab_ref[
                h, g * half : (g + 1) * half, :
            ]


def layout_call(tab, tile):
    rows = tile // 2 * (tile // 128)
    return pl.pallas_call(
        layout_kernel,
        grid=(3,),
        out_shape=jax.ShapeDtypeStruct((3, tile, tile), BF16),
        in_specs=[pl.BlockSpec((2, rows, 128), lambda c: (0, c, 0))],
        out_specs=pl.BlockSpec((1, tile, tile), lambda c: (c, 0, 0)),
        compiler_params=pltpu.CompilerParams(vmem_limit_bytes=VMEM_LIMIT),
        name="layout",
    )(tab)


def on_device(
    basis_values,
    density_matrix,
    points,
    weights,
    intersection,
    basis_index,
    atom_positions,
    shell_blocks,
    shell_widths,
    green,
):
    phi, dens, pts = basis_values[0], density_matrix[0], points[0]
    nz, nx = lax.axis_size("batch_0"), lax.axis_size("batch_1")
    n_row, n_col = lax.axis_size("row"), lax.axis_size("col")
    planes = n_row * n_col
    core = lax.axis_index("batch_2")
    plane = lax.axis_index("col") * n_row + lax.axis_index("row")
    held = nz * nx * planes
    count = intersection.shape[1]
    atoms_col = intersection.reshape(count, 1)
    widths = jnp.broadcast_to(shell_widths.reshape(HALF_S, 2).T.reshape(S, 1), (S, 128))

    sibling_atoms = lax.ppermute(intersection, "batch_2", [(0, 1), (1, 0)])
    slot = jnp.arange(held)
    slot_atom = (slot // planes * 2 + core) * planes + slot % planes

    def found(atoms):
        match = slot_atom[None, :] == atoms.reshape(count, 1)
        return (count + jnp.sum(jnp.where(match, jnp.arange(count)[:, None] - count, 0), axis=0))[None]

    own, sib = found(intersection), found(sibling_atoms)
    mine = lax.dynamic_slice_in_dim(green, plane, 1, 0).reshape(DEG, HALF_S, 2, HALF_S, 2)
    mine = mine.transpose(2, 0, 1, 4, 3).reshape(2 * DEG * HALF_S, S)
    labels = jnp.pad(
        basis_index.reshape(2, -1), ((0, 6), (0, 128 - basis_index.shape[1] // 2)),
        constant_values=-(1 << 20),
    )
    atoms = intersection[0]
    spots = {"z": atoms // (nx * 2 * planes), "x": atoms // (2 * planes) % nx, "y": atoms % planes}
    sizes = {"z": nz, "x": nx, "y": planes}
    starts = []
    for part, order in enumerate(ATOM_ORDERS):
        index = 0
        for axis in order:
            index = index * sizes[axis] + spots[axis]
        starts.append(((atoms // planes % 2 * 3 + part) * held + index) * HALF_S)
    starts = jnp.stack(starts)

    moments = moments_call(
        intersection, shell_blocks, atoms_col, atom_positions, pts, weights, widths, phi, dens
    )
    tab, potential = atoms_call(own, sib, moments, mine, planes)
    quads = field_call(
        starts, intersection, shell_blocks, atoms_col, atom_positions, pts, weights, widths, phi,
        tab.reshape(-1, 128),
    )
    tile = NB // n_row
    matrix = matrix_call(quads, labels, tile, nz * nx)
    return potential.reshape(planes, -1), layout_call(matrix, tile)


def solution(mesh):
    split = (8, 4, 2) if mesh.shape["batch"] == 64 else (mesh.shape["batch"] // 4, 2, 2)
    finer = Mesh(
        mesh.devices.reshape(*split, mesh.shape["row"], mesh.shape["col"]),
        BATCH_ROW_COL,
    )
    placed = (
        P(BATCH_ROW_COL, None, None),
        P(BATCH_ROW_COL, None, None, None),
        P(BATCH_ROW_COL, None, None),
        P(BATCH_ROW_COL, None),
        P(BATCH_ROW_COL, None),
        P(BATCH_ROW_COL, None),
        P(),
        P(),
        P(),
        P(BATCH, None, None),
    )
    return jax.shard_map(
        on_device,
        mesh=finer,
        in_specs=placed,
        out_specs=(P(BATCH, None), P(None, "row", "col")),
        check_vma=False,
    )
```

```python
import math

import jax
import jax.numpy as jnp
from jax import lax
from jax.experimental import pallas as pl
from jax.experimental.pallas import tpu as pltpu
from jax.sharding import Mesh
from jax.sharding import PartitionSpec as P

S = 64
DEG = 8
L = 64
NB = 1536
BATCH = ("batch_0", "batch_1", "batch_2")
BATCH_ROW_COL = ("batch_0", "batch_1", "batch_2", "row", "col")
MESH = pl.DeviceIdType.MESH
F32 = jnp.float32
BF16 = jnp.bfloat16
HALF_S = S // 2
RATE = {"z": 90e3, "x": 90e3, "y": 90e3, "core": 250e3}
HOP = 1.0
ISSUE = 0.05
DIRECT = ""
VMEM_LIMIT = 56 * 1024 * 1024
NT = (((1,), (1,)), ((), ()))


def vmem():
    return pl.BlockSpec(memory_space=pltpu.VMEM)


def smem():
    return pl.BlockSpec(memory_space=pltpu.SMEM)


def as_column(row):
    count = row.shape[1]
    down = lax.broadcasted_iota(jnp.int32, (count, count), 0)
    across = lax.broadcasted_iota(jnp.int32, (count, count), 1)
    return jnp.sum(jnp.where(down == across, row, 0), axis=1, keepdims=True)


def fill_rows(atoms_ref, pos_ref, pts_ref, dist_ref, polar_ref, side_ref):
    count = atoms_ref.shape[1]
    every = pos_ref.shape[1]
    picked = lax.broadcasted_iota(jnp.int32, (count, every), 1) == as_column(atoms_ref[...])
    centre = [
        jnp.sum(jnp.where(picked, pos_ref[d : d + 1, :], 0.0), axis=1, keepdims=True)
        for d in range(3)
    ]
    for group in range(count // 8):
        rows = slice(group * 8, group * 8 + 8)
        dx, dy, dz = [pts_ref[d : d + 1, :] - centre[d][rows] for d in range(3)]
        dist = jnp.sqrt(dx * dx + dy * dy + dz * dz + 0.01)
        inverse = 1.0 / dist
        dist_ref[group] = dist
        for value, ref in ((dz * inverse, polar_ref), (dx * inverse, side_ref)):
            older, newer = jnp.ones_like(value), value
            ref[0, group] = older
            ref[1, group] = newer
            for order in range(2, DEG):
                older, newer = newer, 2.0 * value * newer - older
                ref[order, group] = newer


def shell_rows(widths_ref, lanes):
    row = lax.broadcasted_iota(jnp.int32, (S, lanes), 0)
    shell = jnp.where(row < HALF_S, 2 * row, 2 * (row - HALF_S) + 1)
    middle = shell.astype(F32) * (4.0 / S)
    row = lax.broadcasted_iota(jnp.int32, (S, S), 0)
    order = jnp.where(row < HALF_S, 2 * row, 2 * (row - HALF_S) + 1)
    picked = lax.broadcasted_iota(jnp.int32, (S, S), 1) == order
    widths = jnp.sum(jnp.where(picked, widths_ref[...], 0.0), axis=1, keepdims=True)
    scale = math.sqrt(math.log2(math.e)) / widths
    return shell, middle, jnp.broadcast_to(scale, (S, lanes))


def radial_of(dist, middle, scale, live):
    t = (dist - middle) * scale
    return jnp.where(live, jnp.exp2(-(t * t)), 0.0)


def angular_of(polar_ref, side_ref, group, u, cols):
    side = jnp.concatenate([side_ref[j, group, u : u + 1, cols] for j in range(DEG)], axis=0)
    return jnp.concatenate(
        [side * polar_ref[i, group, u : u + 1, cols] for i in range(DEG)], axis=0
    ).astype(BF16)


def moments_kernel(
    atoms_s, blocks_s, atoms_ref, pos_ref, pts_ref, w_ref, widths_ref, phi_ref, dens_ref,
    out_ref, own_ref, dist_ref, polar_ref, side_ref, wd_ref, scaled_ref, ang_ref, mid_ref, inv_ref,
):
    count = atoms_ref.shape[1]
    held = own_ref.shape[1]
    planes = lax.axis_size("row") * lax.axis_size("col")
    slot = lax.broadcasted_iota(jnp.int32, (count, held), 1)
    wanted = (slot // planes * 2 + lax.axis_index("batch_2")) * planes + lax.rem(slot, planes)
    turn = lax.broadcasted_iota(jnp.int32, (count, held), 0)
    own_ref[...] = count + jnp.sum(
        jnp.where(as_column(atoms_ref[...]) == wanted, turn - count, 0), axis=0, keepdims=True
    )
    points = phi_ref.shape[1]
    fill_rows(atoms_ref, pos_ref, pts_ref, dist_ref, polar_ref, side_ref)
    wide = min(512, points)
    for first in range(0, points, wide):
        cols = slice(first, first + wide)
        phi = phi_ref[:, cols]
        for c in range(3):
            dphi = jnp.dot(dens_ref[c], phi, preferred_element_type=F32)
            total = jnp.sum(phi.astype(F32) * dphi, axis=0, keepdims=True)
            wd_ref[c : c + 1, cols] = total * w_ref[:, cols]
    shell, middle, scale = shell_rows(widths_ref, 128)
    mid_ref[...] = middle
    inv_ref[...] = scale
    out_ref[count] = jnp.zeros((3 * HALF_S, 2 * L), BF16)

    def eight(group, carry):
        for u in range(8):
            k = group * 8 + u
            b = u % 2
            live = shell < 8 * blocks_s[atoms_s[0, k]]
            for first in range(0, points, 128):
                cols = slice(first, first + 128)
                rad = radial_of(dist_ref[group, u : u + 1, cols], mid_ref[...], inv_ref[...], live)
                for c in range(3):
                    part = (rad * wd_ref[c : c + 1, cols]).astype(BF16)
                    for par in range(2):
                        row = par * 96 + c * HALF_S
                        scaled_ref[b, row : row + HALF_S, cols] = part[
                            par * HALF_S : (par + 1) * HALF_S
                        ]
                ang_ref[b, :, cols] = angular_of(polar_ref, side_ref, group, u, cols)
            got = lax.dot_general(scaled_ref[b], ang_ref[b], NT, preferred_element_type=F32)
            out_ref[k] = jnp.concatenate([got[:96], got[96:]], axis=1).astype(BF16)
        return carry

    lax.fori_loop(0, count // 8, eight, 0)


def moments_call(atoms, blocks, atoms_col, pos, pts, w, widths, phi, dens):
    count = atoms.shape[1]
    points = phi.shape[1]
    return pl.pallas_call(
        moments_kernel,
        out_shape=(
            jax.ShapeDtypeStruct((count + 1, 96, 128), BF16),
            jax.ShapeDtypeStruct((1, pos.shape[1] // 2), jnp.int32),
        ),
        in_specs=[smem(), smem()] + [vmem()] * 7,
        out_specs=(vmem(), vmem()),
        scratch_shapes=[
            pltpu.VMEM((count // 8, 8, points), F32),
            pltpu.VMEM((DEG, count // 8, 8, points), F32),
            pltpu.VMEM((DEG, count // 8, 8, points), F32),
            pltpu.VMEM((8, points), F32),
            pltpu.VMEM((2, 192, points), BF16),
            pltpu.VMEM((2, L, points), BF16),
            pltpu.VMEM((S, 128), F32),
            pltpu.VMEM((S, 128), F32),
        ],
        compiler_params=pltpu.CompilerParams(vmem_limit_bytes=VMEM_LIMIT),
        cost_estimate=pl.CostEstimate(flops=4_000_000_000, bytes_accessed=3_000_000, transcendentals=4_000_000),
        name="moments",
    )(atoms, blocks, atoms_col, pos, pts, w, widths, phi, dens)


class Rings:
    def __init__(self, send, recv):
        self.send, self.recv = send, recv
        self.used = 0
        self.started = []
        self.now = 0.0
        self.free = {}
        self.lands = {}
        self.tasks = []
        self.core = lax.axis_index("batch_2")
        self.turn = 1 - 2 * self.core
        rows = lax.axis_size("row")
        self.size = {
            "z": lax.axis_size("batch_0"),
            "x": lax.axis_size("batch_1"),
            "y": rows * lax.axis_size("col"),
        }
        self.at = {
            "z": lax.axis_index("batch_0"),
            "x": lax.axis_index("batch_1"),
            "y": lax.axis_index("col") * rows + lax.axis_index("row"),
        }

    def place(self, axis, shift):
        n = self.size[axis]
        return lax.rem(self.at[axis] + shift + 2 * n, n)

    def device(self, axis, shift):
        spot = self.place(axis, shift)
        if axis == "z":
            return {"batch_0": spot}
        if axis == "x":
            return {"batch_1": spot}
        rows = lax.axis_size("row")
        return {"row": lax.rem(spot, rows), "col": spot // rows}

    def sibling(self):
        return {"batch_2": 1 - self.core}

    def greet(self, axes, others=()):
        barrier = pltpu.get_barrier_semaphore()
        greeted = 0
        for axis in axes:
            for shift in range(1, self.size[axis]):
                pl.semaphore_signal(
                    barrier, inc=1, device_id=self.device(axis, shift), device_id_type=MESH
                )
                greeted += 1
        for other in others:
            pl.semaphore_signal(barrier, inc=1, device_id=other, device_id_type=MESH)
            greeted += 1
        pl.semaphore_wait(barrier, greeted)

    def ticket(self):
        self.used += 1
        return self.used - 1

    def copy(self, src, dst, ticket, device, link="core", hops=1):
        made = pltpu.make_async_remote_copy(
            src_ref=src, dst_ref=dst, send_sem=self.send.at[ticket],
            recv_sem=self.recv.at[ticket], device_id=device, device_id_type=MESH,
        )
        made.start()
        self.started.append(made)
        took = hops * math.prod(src.shape) * 2 / RATE[link]
        self.free[link] = max(self.free.get(link, 0.0), self.now) + took
        self.lands[ticket] = self.free[link] + HOP
        self.now += ISSUE

    def spawn(self, work):
        task = [work, None]
        self.tasks.append(task)
        self.step(task)
        return task

    def step(self, task):
        try:
            task[1] = next(task[0])
        except StopIteration:
            self.tasks.remove(task)

    def ready(self, task):
        wanted = task[1]
        if isinstance(wanted, list):
            return math.inf if any(other in self.tasks for other in wanted) else self.now
        return self.lands.get(wanted, math.inf)

    def run(self):
        while self.tasks:
            task = min(self.tasks, key=self.ready)
            self.now = max(self.now, self.ready(task)) + ISSUE
            self.step(task)

    def arrive(self, dst, ticket):
        pltpu.make_async_remote_copy(
            src_ref=dst, dst_ref=dst, send_sem=self.send.at[ticket],
            recv_sem=self.recv.at[ticket], device_id=self.sibling(), device_id_type=MESH,
        ).wait_recv()

    def finish(self):
        for made in self.started:
            made.wait_send()

    def reduce(self, buf, base, rows, axis, slots, spot):
        n = self.size[axis]
        if n == 1:
            return
        here = self.at[axis]
        lanes = [(1, n // 2), (-1, n // 2 - 1)]
        tickets = [[self.ticket() for _ in range(steps)] for _, steps in lanes]
        places = []
        for _, steps in lanes:
            places.append([spot + rows * k for k in range(steps)])
            spot += rows * steps

        def own(shift):
            return pl.ds(pl.multiple_of(base + self.place(axis, shift) * rows, 16), rows)

        def chain(lane, way, steps):
            for t in range(steps):
                mine = own(-way * self.turn * (steps - t))
                if t == 0:
                    source = buf.at[mine]
                else:
                    source = slots.at[pl.ds(places[lane][t - 1], rows)]
                    yield tickets[lane][t - 1]
                    self.arrive(source, tickets[lane][t - 1])
                    source[...] = (source[...].astype(F32) + buf[mine, :].astype(F32)).astype(BF16)
                self.copy(
                    source, slots.at[pl.ds(places[lane][t], rows)], tickets[lane][t],
                    self.device(axis, -way * self.turn), axis,
                )

        for lane, (way, steps) in enumerate(lanes):
            if steps:
                self.spawn(chain(lane, way, steps))
        total = buf[own(0), :].astype(F32)
        for lane, (way, steps) in enumerate(lanes):
            if steps:
                source = slots.at[pl.ds(places[lane][-1], rows)]
                yield tickets[lane][-1]
                self.arrive(source, tickets[lane][-1])
                total = total + source[...].astype(F32)
        buf[own(0), :] = total.astype(BF16)

    def far_first(self, axis):
        return sorted(range(1, self.size[axis]), key=lambda k: -min(k, self.size[axis] - k))

    def reduce_direct(self, buf, base, rows, axis, slots, spot):
        waits = []
        for k in self.far_first(axis):
            ticket = self.ticket()
            start = pl.multiple_of(base + self.place(axis, k * self.turn) * rows, 16)
            slot = slots.at[pl.ds(spot + (k - 1) * rows, rows)]
            hops = min(k, self.size[axis] - k)
            self.copy(
                buf.at[pl.ds(start, rows)], slot, ticket,
                self.device(axis, k * self.turn), axis, hops,
            )
            waits.append((ticket, slot))
        here = pl.ds(pl.multiple_of(base + self.at[axis] * rows, 16), rows)
        total = buf[here, :].astype(F32)
        for ticket, slot in waits:
            yield ticket
            self.arrive(slot, ticket)
            total = total + slot[...].astype(F32)
        buf[here, :] = total.astype(BF16)

    def gather_direct(self, buf, base, rows, axis, arrived=None):
        def chunk(shift):
            start = pl.multiple_of(base + self.place(axis, shift * self.turn) * rows, 16)
            return buf.at[pl.ds(start, rows)]

        waits = []
        for k in self.far_first(axis):
            ticket = self.ticket()
            hops = min(k, self.size[axis] - k)
            self.copy(
                chunk(0), chunk(0), ticket, self.device(axis, k * self.turn), axis, hops
            )
            waits.append((ticket, k))
        if arrived:
            arrived(0)
        for ticket, k in waits:
            yield ticket
            self.arrive(chunk(-k), ticket)
            if arrived:
                arrived(-k)

    def gather(self, buf, base, rows, axis, arrived=None):
        n = self.size[axis]
        if n == 1:
            if arrived:
                arrived(0)
            return
        lanes = [(1, n // 2), (-1, n // 2 - 1)]
        tickets = [[self.ticket() for _ in range(steps)] for _, steps in lanes]

        def chunk(shift):
            start = pl.multiple_of(base + self.place(axis, shift) * rows, 16)
            return buf.at[pl.ds(start, rows)]

        def chain(lane, way, steps):
            for t in range(steps + 1):
                block = chunk(way * self.turn * t)
                if t > 0:
                    yield tickets[lane][t - 1]
                    self.arrive(block, tickets[lane][t - 1])
                if t < steps:
                    self.copy(
                        block, block, tickets[lane][t], self.device(axis, -way * self.turn), axis
                    )
                if t > 0 and arrived:
                    arrived(way * t)

        chains = [
            self.spawn(chain(lane, way, steps)) for lane, (way, steps) in enumerate(lanes) if steps
        ]
        if arrived:
            arrived(0)
        yield chains


def spread_out(rings, tab, base, total_rows, axes, forwards):
    mine = tab.at[rings.core]
    levels = []
    rows, start = total_rows, base
    for axis in axes:
        rows //= rings.size[axis]
        levels.append((axis, start, rows))
        start = start + rings.at[axis] * rows
    for depth in reversed(range(len(levels))):
        axis, first, rows = levels[depth]

        def forward(shift, axis=axis, first=first, rows=rows):
            ticket = rings.ticket()
            signed = shift * rings.turn
            here = pl.ds(pl.multiple_of(first + rings.place(axis, signed) * rows, 16), rows)
            there = pl.ds(pl.multiple_of(first + rings.place(axis, -signed) * rows, 16), rows)
            rings.copy(tab.at[rings.core, here], tab.at[rings.core, here], ticket, rings.sibling())
            forwards.append((tab.at[1 - rings.core, there], ticket))

        step = rings.gather_direct if depth or axis in DIRECT else rings.gather
        yield from step(mine, first, rows, axis, forward if depth == 0 else None)


def collect(rings, buf, base, total_rows, axes, slots, spot):
    rows, start = total_rows, base
    for depth, axis in enumerate(axes):
        rows //= rings.size[axis]
        step = rings.reduce_direct if depth or axis in DIRECT else rings.reduce
        yield from step(buf, start, rows, axis, slots, spot)
        spot += rows * (rings.size[axis] - 1)
        start = start + rings.at[axis] * rows


def chunk_start(rings, base, total_rows, axes):
    rows, start = total_rows, base
    for axis in axes:
        rows //= rings.size[axis]
        start = start + rings.at[axis] * rows
    return start, rows


ATOM_ORDERS = (("y", "x", "z"), ("z", "y", "x"), ("x", "y", "z"))


def atoms_kernel(
    own_s, sib_s, mom_ref, green_ref, tab_ref, pot_ref, dense, slots, other, send, recv
):
    rings = Rings(send, recv)
    nz, nx, ny = (rings.size[a] for a in "zxy")
    held = nz * nx * ny
    part_rows = held * HALF_S
    rings.greet("zxy", [rings.sibling()])
    ticket = rings.ticket()
    rings.copy(mom_ref, other, ticket, rings.sibling())
    rings.arrive(other, ticket)

    def place(slot, order):
        spots = {"z": slot // (nx * ny), "x": lax.rem(slot // ny, nx), "y": lax.rem(slot, ny)}
        index = 0
        for axis in order:
            index = index * rings.size[axis] + spots[axis]
        return index

    def fill(slot, carry):
        value = mom_ref[own_s[0, slot]] + other[sib_s[0, slot]]
        for part, order in enumerate(ATOM_ORDERS):
            row = pl.multiple_of(part * part_rows + place(slot, order) * HALF_S, 32)
            dense[pl.ds(row, HALF_S), :] = value[part * HALF_S : (part + 1) * HALF_S]
        return carry

    lax.fori_loop(0, held, fill, 0, unroll=4)
    forwards = []
    green = green_ref[...]
    column = lax.broadcasted_iota(jnp.int32, (DEG, HALF_S, L), 2) // DEG
    layer = lax.broadcasted_iota(jnp.int32, (DEG, HALF_S, L), 0)

    def task(part):
        order = ATOM_ORDERS[part]
        base = part * part_rows
        yield from collect(rings, dense, base, part_rows, order, slots, base)
        start, rows = chunk_start(rings, base, part_rows, order)
        here = pl.ds(pl.multiple_of(start, 32), rows)
        charges = dense[here, :].astype(F32)
        stacked = jnp.concatenate([charges[:, :L], charges[:, L:]], axis=0).astype(BF16)
        result = jnp.dot(green, stacked, preferred_element_type=F32)
        sides = []
        for par in range(2):
            block = result[par * DEG * HALF_S : (par + 1) * DEG * HALF_S].reshape(DEG, HALF_S, L)
            sides.append(jnp.sum(jnp.where(column == layer, block, 0.0), axis=0))
        tab_ref[rings.core, here, :] = jnp.concatenate(sides, axis=1).astype(BF16)
        yield from spread_out(rings, tab_ref, base, part_rows, order, forwards)

    for part in range(3):
        rings.spawn(task(part))
    rings.run()
    for slot in range(ny):
        for part, order in enumerate(ATOM_ORDERS):
            index = 0
            for axis in order:
                index = index * rings.size[axis] + (slot if axis == "y" else rings.at[axis])
            row = pl.multiple_of(part * part_rows + index * HALF_S, 32)
            pot_ref[slot, part * HALF_S : (part + 1) * HALF_S, :] = tab_ref[
                rings.core, pl.ds(row, HALF_S), :
            ]
    for block, ticket in forwards:
        rings.arrive(block, ticket)
    rings.finish()


def atoms_call(own, sib, moments, green, planes):
    held = own.shape[1]
    return pl.pallas_call(
        atoms_kernel,
        out_shape=(
            jax.ShapeDtypeStruct((2, 3 * held * HALF_S, 128), BF16),
            jax.ShapeDtypeStruct((planes, 96, 128), BF16),
        ),
        in_specs=[smem(), smem(), vmem(), vmem()],
        out_specs=(vmem(), vmem()),
        scratch_shapes=[
            pltpu.VMEM((3 * held * HALF_S, 128), BF16),
            pltpu.VMEM((3 * held * HALF_S, 128), BF16),
            pltpu.VMEM(moments.shape, BF16),
            pltpu.SemaphoreType.DMA((128,)),
            pltpu.SemaphoreType.DMA((128,)),
        ],
        compiler_params=pltpu.CompilerParams(
            vmem_limit_bytes=VMEM_LIMIT, collective_id=0, has_side_effects=True
        ),
        cost_estimate=pl.CostEstimate(flops=100_000_000, bytes_accessed=60_000_000, transcendentals=0),
        name="atoms",
    )(own, sib, moments, green)


def field_kernel(
    atoms_s, blocks_s, atoms_ref, pos_ref, pts_ref, w_ref, widths_ref, phi_ref, tab_ref,
    out_ref, dist_ref, polar_ref, side_ref, acc_ref, operand_ref, pad_ref, mid_ref, inv_ref,
):
    count = atoms_ref.shape[1]
    points = phi_ref.shape[1]
    basis = phi_ref.shape[0]
    piece = basis // 2
    nx, planes = lax.axis_size("batch_1"), lax.axis_size("row") * lax.axis_size("col")
    sizes = {"z": lax.axis_size("batch_0"), "x": nx, "y": planes}
    fill_rows(atoms_ref, pos_ref, pts_ref, dist_ref, polar_ref, side_ref)
    wide = min(256, points)
    shell, middle, scale = shell_rows(widths_ref, wide)
    mid_ref[...] = middle
    inv_ref[...] = scale
    acc_ref[...] = jnp.zeros_like(acc_ref)

    def eight(group, carry):
        for u in range(8):
            k = group * 8 + u
            atom = atoms_s[0, k]
            live = shell < 8 * blocks_s[atom]
            spots = {
                "z": atom // (nx * 2 * planes),
                "x": lax.rem(atom // (2 * planes), nx),
                "y": lax.rem(atom, planes),
            }
            packed = []
            for part, order in enumerate(ATOM_ORDERS):
                index = lax.rem(atom // planes, 2) * 3 + part
                for axis in order:
                    index = index * sizes[axis] + spots[axis]
                packed.append(tab_ref[pl.ds(pl.multiple_of(index * HALF_S, 32), HALF_S), :])
            packed = jnp.concatenate(packed, axis=0)
            table = jnp.concatenate([packed[:, :L], packed[:, L:]], axis=0)
            for first in range(0, points, wide):
                cols = slice(first, first + wide)
                ang = angular_of(polar_ref, side_ref, group, u, cols)
                spread = jnp.dot(table, ang, preferred_element_type=F32)
                rad = radial_of(dist_ref[group, u : u + 1, cols], mid_ref[...], inv_ref[...], live)
                for c in range(3):
                    total = acc_ref[c, :, cols]
                    for par in range(2):
                        row = par * 96 + c * HALF_S
                        prod = spread[row : row + HALF_S] * rad[par * HALF_S : (par + 1) * HALF_S]
                        for g in range(0, HALF_S, 8):
                            total = total + prod[g : g + 8]
                    acc_ref[c, :, cols] = total
        return carry

    lax.fori_loop(0, count // 8, eight, 0)
    for q in range(2):
        pad_ref[q, :piece, :] = phi_ref[q * piece : (q + 1) * piece, :]
        pad_ref[q, piece:, :] = jnp.zeros((128 - piece, points), BF16)
    for c in range(3):
        field = jnp.sum(acc_ref[c], axis=0, keepdims=True) * w_ref[...]
        for first in range(0, points, wide):
            cols = slice(first, first + wide)
            operand_ref[:, cols] = (phi_ref[:, cols].astype(F32) * field[:, cols]).astype(BF16)
        for q in range(2):
            local = lax.dot_general(
                operand_ref[...], pad_ref[q], NT, preferred_element_type=F32
            ).astype(BF16)
            for r in range(2):
                out_ref[r * 2 + q, :, c * 128 : (c + 1) * 128] = local[r * piece : (r + 1) * piece]


def field_call(atoms, blocks, atoms_col, pos, pts, w, widths, phi, tab):
    count = atoms.shape[1]
    basis, points = phi.shape
    wide = min(256, points)
    return pl.pallas_call(
        field_kernel,
        out_shape=jax.ShapeDtypeStruct((4, basis // 2, 384), BF16),
        in_specs=[smem()] * 2 + [vmem()] * 7,
        out_specs=vmem(),
        scratch_shapes=[
            pltpu.VMEM((count // 8, 8, points), F32),
            pltpu.VMEM((DEG, count // 8, 8, points), F32),
            pltpu.VMEM((DEG, count // 8, 8, points), F32),
            pltpu.VMEM((3, 8, points), F32),
            pltpu.VMEM((basis, points), BF16),
            pltpu.VMEM((2, 128, points), BF16),
            pltpu.VMEM((S, wide), F32),
            pltpu.VMEM((S, wide), F32),
        ],
        compiler_params=pltpu.CompilerParams(vmem_limit_bytes=VMEM_LIMIT),
        cost_estimate=pl.CostEstimate(flops=4_000_000_000, bytes_accessed=8_000_000, transcendentals=4_000_000),
        name="field",
    )(atoms, blocks, atoms_col, pos, pts, w, widths, phi, tab)


TILE_ORDERS = (("z", "x"), ("x", "z"))


def matrix_kernel(quads_ref, label_ref, tab_ref, flat, slots, got, marks, placed, hit, send, recv):
    rings = Rings(send, recv)
    row, col, core = (lax.axis_index(a) for a in ("row", "col", "batch_2"))
    n_row, n_col = lax.axis_size("row"), lax.axis_size("col")
    piece = quads_ref.shape[1]
    tile = hit.shape[0]
    half = tile // 2
    me = (core * n_row + row) * n_col + col
    shifts = [
        (dc, dr, dl) for dc in range(2) for dr in range(n_row) for dl in range(n_col)
    ][1:]

    def peer(shift):
        return {
            "batch_2": lax.rem(core + shift[0], 2),
            "row": lax.rem(row + shift[1], n_row),
            "col": lax.rem(col + shift[2], n_col),
        }

    rings.greet("zx", [peer(shift) for shift in shifts])
    waits = []
    for shift in shifts:
        to = peer(shift)
        first, second = rings.ticket(), rings.ticket()
        rings.copy(label_ref, marks.at[me], first, to)
        rings.copy(quads_ref.at[to["row"] * 2 + to["col"]], got.at[me], second, to)
        source = (to["batch_2"] * n_row + to["row"]) * n_col + to["col"]
        waits.append((marks.at[source], first, got.at[source], second))
    marks[me] = label_ref[...]
    got[me] = quads_ref[row * 2 + col]
    padded = flat.shape[0] - 3 * half * (tile // 128)
    flat[flat.shape[0] - padded :, :] = jnp.zeros((padded, 128), BF16)
    for mark, first, block, second in waits:
        rings.arrive(mark, first)
        rings.arrive(block, second)
    sources = 2 * n_row * n_col
    for s in range(sources):
        label = marks[s]
        rows_at = jnp.where(row == 0, label[0:1, :], label[1:2, :]) - row * tile - core * half
        cols_at = jnp.where(col == 0, label[0:1, :], label[1:2, :]) - col * tile
        row_hit = lax.broadcasted_iota(jnp.int32, (half, 128), 0) == rows_at
        row_hit = jnp.where(row_hit, 1.0, 0.0).astype(BF16)[:, :piece]
        spread = jnp.dot(row_hit, got[s], preferred_element_type=F32).astype(BF16)
        for c in range(3):
            placed[c * half : (c + 1) * half, s * 128 : (s + 1) * 128] = spread[
                :, c * 128 : (c + 1) * 128
            ]
        col_hit = lax.broadcasted_iota(jnp.int32, (tile, 128), 0) == cols_at
        hit[:, s * 128 : (s + 1) * 128] = jnp.where(col_hit, 1.0, 0.0).astype(BF16)
    groups = tile // 128
    for c in range(3):
        for j in range(tile // 256):
            block = lax.dot_general(
                placed[c * half : (c + 1) * half, :], hit[j * 256 : (j + 1) * 256, :], NT,
                preferred_element_type=F32,
            ).astype(BF16)
            for h in range(2):
                start = (c * groups + 2 * j + h) * half
                flat[start : start + half, :] = block[:, h * 128 : (h + 1) * 128]
    part_rows = flat.shape[0] // 2
    forwards = []

    def task(part):
        order = TILE_ORDERS[part]
        base = part * part_rows
        yield from collect(rings, flat, base, part_rows, order, slots, base)
        start, rows = chunk_start(rings, base, part_rows, order)
        here = pl.ds(pl.multiple_of(start, 16), rows)
        tab_ref[rings.core, here, :] = flat[here, :]
        yield from spread_out(rings, tab_ref, base, part_rows, order, forwards)

    for part in range(2):
        rings.spawn(task(part))
    rings.run()
    for block, ticket in forwards:
        rings.arrive(block, ticket)
    rings.finish()


def matrix_call(quads, labels, tile, ring_devices):
    half = tile // 2
    used = 3 * half * (tile // 128)
    unit = 2 * 16 * ring_devices
    rows = -(-used // unit) * unit
    sources = 8
    piece = quads.shape[1]
    return pl.pallas_call(
        matrix_kernel,
        out_shape=jax.ShapeDtypeStruct((2, rows, 128), BF16),
        in_specs=[vmem(), vmem()],
        out_specs=vmem(),
        scratch_shapes=[
            pltpu.VMEM((rows, 128), BF16),
            pltpu.VMEM((rows, 128), BF16),
            pltpu.VMEM((sources, piece, 384), BF16),
            pltpu.VMEM((sources, 8, 128), jnp.int32),
            pltpu.VMEM((3 * half, sources * 128), BF16),
            pltpu.VMEM((tile, sources * 128), BF16),
            pltpu.SemaphoreType.DMA((80,)),
            pltpu.SemaphoreType.DMA((80,)),
        ],
        compiler_params=pltpu.CompilerParams(
            vmem_limit_bytes=VMEM_LIMIT, collective_id=1, has_side_effects=True
        ),
        cost_estimate=pl.CostEstimate(flops=2_000_000_000, bytes_accessed=60_000_000, transcendentals=0),
        name="matrix",
    )(quads, labels)


def layout_kernel(tab_ref, out_ref):
    tile = out_ref.shape[2]
    half = tile // 2
    for h in range(2):
        for g in range(tile // 128):
            out_ref[0, h * half : (h + 1) * half, g * 128 : (g + 1) * 128] = tab_ref[
                h, g * half : (g + 1) * half, :
            ]


def layout_call(tab, tile):
    rows = tile // 2 * (tile // 128)
    return pl.pallas_call(
        layout_kernel,
        grid=(3,),
        out_shape=jax.ShapeDtypeStruct((3, tile, tile), BF16),
        in_specs=[pl.BlockSpec((2, rows, 128), lambda c: (0, c, 0))],
        out_specs=pl.BlockSpec((1, tile, tile), lambda c: (c, 0, 0)),
        compiler_params=pltpu.CompilerParams(vmem_limit_bytes=VMEM_LIMIT),
        name="layout",
    )(tab)


def on_device(
    basis_values,
    density_matrix,
    points,
    weights,
    intersection,
    basis_index,
    atom_positions,
    shell_blocks,
    shell_widths,
    green,
):
    phi, dens, pts = basis_values[0], density_matrix[0], points[0]
    nz, nx = lax.axis_size("batch_0"), lax.axis_size("batch_1")
    n_row, n_col = lax.axis_size("row"), lax.axis_size("col")
    planes = n_row * n_col
    core = lax.axis_index("batch_2")
    plane = lax.axis_index("col") * n_row + lax.axis_index("row")
    held = nz * nx * planes
    count = intersection.shape[1]
    widths = shell_widths.reshape(1, S)

    sibling_atoms = lax.ppermute(intersection, "batch_2", [(0, 1), (1, 0)])
    slot = jnp.arange(held)
    slot_atom = (slot // planes * 2 + core) * planes + slot % planes

    def found(atoms):
        match = slot_atom[None, :] == atoms.reshape(count, 1)
        return (count + jnp.sum(jnp.where(match, jnp.arange(count)[:, None] - count, 0), axis=0))[None]

    sib = found(sibling_atoms)
    mine = lax.dynamic_slice_in_dim(green, plane, 1, 0).reshape(DEG, HALF_S, 2, HALF_S, 2)
    mine = mine.transpose(2, 0, 1, 4, 3).reshape(2 * DEG * HALF_S, S)
    labels = jnp.pad(
        basis_index.reshape(2, -1), ((0, 6), (0, 128 - basis_index.shape[1] // 2)),
        constant_values=-(1 << 20),
    )
    moments, own = moments_call(
        intersection, shell_blocks, intersection, atom_positions, pts, weights, widths, phi, dens
    )
    tab, potential = atoms_call(own, sib, moments, mine, planes)
    quads = field_call(
        intersection, shell_blocks, intersection, atom_positions, pts, weights, widths, phi,
        tab.reshape(-1, 128),
    )
    tile = NB // n_row
    matrix = matrix_call(quads, labels, tile, nz * nx)
    return potential.reshape(planes, -1), layout_call(matrix, tile)


def solution(mesh):
    split = (8, 4, 2) if mesh.shape["batch"] == 64 else (mesh.shape["batch"] // 4, 2, 2)
    finer = Mesh(
        mesh.devices.reshape(*split, mesh.shape["row"], mesh.shape["col"]),
        BATCH_ROW_COL,
    )
    placed = (
        P(BATCH_ROW_COL, None, None),
        P(BATCH_ROW_COL, None, None, None),
        P(BATCH_ROW_COL, None, None),
        P(BATCH_ROW_COL, None),
        P(BATCH_ROW_COL, None),
        P(BATCH_ROW_COL, None),
        P(),
        P(),
        P(),
        P(BATCH, None, None),
    )
    return jax.shard_map(
        on_device,
        mesh=finer,
        in_specs=placed,
        out_specs=(P(BATCH, None), P(None, "row", "col")),
        check_vma=False,
    )
```

```python
import math

import jax
import jax.numpy as jnp
from jax import lax
from jax.experimental import pallas as pl
from jax.experimental.pallas import tpu as pltpu
from jax.sharding import Mesh
from jax.sharding import PartitionSpec as P

S = 64
DEG = 8
L = 64
NB = 1536
BATCH = ("batch_0", "batch_1", "batch_2")
BATCH_ROW_COL = ("batch_0", "batch_1", "batch_2", "row", "col")
MESH = pl.DeviceIdType.MESH
F32 = jnp.float32
BF16 = jnp.bfloat16
HALF_S = S // 2
RATE = {"z": 90e3, "x": 90e3, "y": 90e3, "core": 250e3}
HOP = 1.0
ISSUE = 0.05
DIRECT = ""
VMEM_LIMIT = 56 * 1024 * 1024
NT = (((1,), (1,)), ((), ()))


def vmem():
    return pl.BlockSpec(memory_space=pltpu.VMEM)


def smem():
    return pl.BlockSpec(memory_space=pltpu.SMEM)


def as_column(row):
    count = row.shape[1]
    down = lax.broadcasted_iota(jnp.int32, (count, count), 0)
    across = lax.broadcasted_iota(jnp.int32, (count, count), 1)
    return jnp.sum(jnp.where(down == across, row, 0), axis=1, keepdims=True)


def fill_rows(atoms_ref, pos_ref, pts_ref, dist_ref, polar_ref, side_ref):
    count = atoms_ref.shape[1]
    every = pos_ref.shape[1]
    picked = lax.broadcasted_iota(jnp.int32, (count, every), 1) == as_column(atoms_ref[...])
    centre = [
        jnp.sum(jnp.where(picked, pos_ref[d : d + 1, :], 0.0), axis=1, keepdims=True)
        for d in range(3)
    ]
    for group in range(count // 8):
        rows = slice(group * 8, group * 8 + 8)
        dx, dy, dz = [pts_ref[d : d + 1, :] - centre[d][rows] for d in range(3)]
        dist = jnp.sqrt(dx * dx + dy * dy + dz * dz + 0.01)
        inverse = 1.0 / dist
        dist_ref[group] = dist
        for value, ref in ((dz * inverse, polar_ref), (dx * inverse, side_ref)):
            older, newer = jnp.ones_like(value), value
            ref[0, group] = older
            ref[1, group] = newer
            for order in range(2, DEG):
                older, newer = newer, 2.0 * value * newer - older
                ref[order, group] = newer


def shell_rows(widths_ref, lanes):
    row = lax.broadcasted_iota(jnp.int32, (S, lanes), 0)
    shell = jnp.where(row < HALF_S, 2 * row, 2 * (row - HALF_S) + 1)
    middle = shell.astype(F32) * (4.0 / S)
    row = lax.broadcasted_iota(jnp.int32, (S, S), 0)
    order = jnp.where(row < HALF_S, 2 * row, 2 * (row - HALF_S) + 1)
    picked = lax.broadcasted_iota(jnp.int32, (S, S), 1) == order
    widths = jnp.sum(jnp.where(picked, widths_ref[...], 0.0), axis=1, keepdims=True)
    scale = math.sqrt(math.log2(math.e)) / widths
    return shell, middle, jnp.broadcast_to(scale, (S, lanes))


def radial_of(dist, middle, scale, live):
    t = (dist - middle) * scale
    return jnp.where(live, jnp.exp2(-(t * t)), 0.0)


def angular_of(polar_ref, side_ref, group, u, cols):
    side = jnp.concatenate([side_ref[j, group, u : u + 1, cols] for j in range(DEG)], axis=0)
    return jnp.concatenate(
        [side * polar_ref[i, group, u : u + 1, cols] for i in range(DEG)], axis=0
    ).astype(BF16)


def moments_stage(
    atoms_s, blocks_s, atoms_ref, pos_ref, pts_ref, w_ref, widths_ref, phi_ref, dens_ref,
    out_ref, dist_ref, polar_ref, side_ref, wd_ref, scaled_ref, ang_ref, mid_ref, inv_ref,
):
    count = atoms_ref.shape[1]
    points = phi_ref.shape[1]
    fill_rows(atoms_ref, pos_ref, pts_ref, dist_ref, polar_ref, side_ref)
    wide = min(512, points)
    for first in range(0, points, wide):
        cols = slice(first, first + wide)
        phi = phi_ref[:, cols]
        for c in range(3):
            dphi = jnp.dot(dens_ref[c], phi, preferred_element_type=F32)
            total = jnp.sum(phi.astype(F32) * dphi, axis=0, keepdims=True)
            wd_ref[c : c + 1, cols] = total * w_ref[:, cols]
    shell, middle, scale = shell_rows(widths_ref, mid_ref.shape[1])
    shell = shell[:, :128]
    mid_ref[...] = middle
    inv_ref[...] = scale
    out_ref[count] = jnp.zeros((3 * HALF_S, 2 * L), BF16)

    def eight(group, carry):
        for u in range(8):
            k = group * 8 + u
            b = u % 2
            live = shell < 8 * blocks_s[atoms_s[0, k]]
            for first in range(0, points, 128):
                cols = slice(first, first + 128)
                rad = radial_of(
                    dist_ref[group, u : u + 1, cols], mid_ref[:, :128], inv_ref[:, :128], live
                )
                for c in range(3):
                    part = (rad * wd_ref[c : c + 1, cols]).astype(BF16)
                    for par in range(2):
                        row = par * 96 + c * HALF_S
                        scaled_ref[b, row : row + HALF_S, cols] = part[
                            par * HALF_S : (par + 1) * HALF_S
                        ]
                ang_ref[b, :, cols] = angular_of(polar_ref, side_ref, group, u, cols)
            got = lax.dot_general(scaled_ref[b], ang_ref[b], NT, preferred_element_type=F32)
            out_ref[k] = jnp.concatenate([got[:96], got[96:]], axis=1).astype(BF16)
        return carry

    lax.fori_loop(0, count // 8, eight, 0)


class Rings:
    def __init__(self, send, recv):
        self.send, self.recv = send, recv
        self.used = 0
        self.started = []
        self.now = 0.0
        self.free = {}
        self.lands = {}
        self.tasks = []
        self.core = lax.axis_index("batch_2")
        self.turn = 1 - 2 * self.core
        rows = lax.axis_size("row")
        self.size = {
            "z": lax.axis_size("batch_0"),
            "x": lax.axis_size("batch_1"),
            "y": rows * lax.axis_size("col"),
        }
        self.at = {
            "z": lax.axis_index("batch_0"),
            "x": lax.axis_index("batch_1"),
            "y": lax.axis_index("col") * rows + lax.axis_index("row"),
        }

    def place(self, axis, shift):
        n = self.size[axis]
        return lax.rem(self.at[axis] + shift + 2 * n, n)

    def device(self, axis, shift):
        spot = self.place(axis, shift)
        if axis == "z":
            return {"batch_0": spot}
        if axis == "x":
            return {"batch_1": spot}
        rows = lax.axis_size("row")
        return {"row": lax.rem(spot, rows), "col": spot // rows}

    def sibling(self):
        return {"batch_2": 1 - self.core}

    def greet(self, axes, others=()):
        barrier = pltpu.get_barrier_semaphore()
        greeted = 0
        for axis in axes:
            for shift in range(1, self.size[axis]):
                pl.semaphore_signal(
                    barrier, inc=1, device_id=self.device(axis, shift), device_id_type=MESH
                )
                greeted += 1
        for other in others:
            pl.semaphore_signal(barrier, inc=1, device_id=other, device_id_type=MESH)
            greeted += 1
        return greeted

    def ticket(self):
        self.used += 1
        return self.used - 1

    def copy(self, src, dst, ticket, device, link="core", hops=1):
        made = pltpu.make_async_remote_copy(
            src_ref=src, dst_ref=dst, send_sem=self.send.at[ticket],
            recv_sem=self.recv.at[ticket], device_id=device, device_id_type=MESH,
        )
        made.start()
        self.started.append(made)
        took = hops * math.prod(src.shape) * 2 / RATE[link]
        self.free[link] = max(self.free.get(link, 0.0), self.now) + took
        self.lands[ticket] = self.free[link] + HOP
        self.now += ISSUE

    def spawn(self, work):
        task = [work, None]
        self.tasks.append(task)
        self.step(task)
        return task

    def step(self, task):
        try:
            task[1] = next(task[0])
        except StopIteration:
            self.tasks.remove(task)

    def ready(self, task):
        wanted = task[1]
        if isinstance(wanted, list):
            return math.inf if any(other in self.tasks for other in wanted) else self.now
        return self.lands.get(wanted, math.inf)

    def run(self):
        while self.tasks:
            task = min(self.tasks, key=self.ready)
            self.now = max(self.now, self.ready(task)) + ISSUE
            self.step(task)

    def arrive(self, dst, ticket):
        pltpu.make_async_remote_copy(
            src_ref=dst, dst_ref=dst, send_sem=self.send.at[ticket],
            recv_sem=self.recv.at[ticket], device_id=self.sibling(), device_id_type=MESH,
        ).wait_recv()

    def finish(self):
        for made in self.started:
            made.wait_send()

    def reduce(self, buf, base, rows, axis, slots, spot):
        n = self.size[axis]
        if n == 1:
            return
        here = self.at[axis]
        lanes = [(1, n // 2), (-1, n // 2 - 1)]
        tickets = [[self.ticket() for _ in range(steps)] for _, steps in lanes]
        places = []
        for _, steps in lanes:
            places.append([spot + rows * k for k in range(steps)])
            spot += rows * steps

        def own(shift):
            return pl.ds(base + self.place(axis, shift) * rows, rows)

        def chain(lane, way, steps):
            for t in range(steps):
                mine = own(-way * self.turn * (steps - t))
                if t == 0:
                    source = buf.at[mine]
                else:
                    source = slots.at[pl.ds(places[lane][t - 1], rows)]
                    yield tickets[lane][t - 1]
                    self.arrive(source, tickets[lane][t - 1])
                    source[...] = (source[...].astype(F32) + buf[mine].astype(F32)).astype(BF16)
                self.copy(
                    source, slots.at[pl.ds(places[lane][t], rows)], tickets[lane][t],
                    self.device(axis, -way * self.turn), axis,
                )

        for lane, (way, steps) in enumerate(lanes):
            if steps:
                self.spawn(chain(lane, way, steps))
        total = buf[own(0)].astype(F32)
        for lane, (way, steps) in enumerate(lanes):
            if steps:
                source = slots.at[pl.ds(places[lane][-1], rows)]
                yield tickets[lane][-1]
                self.arrive(source, tickets[lane][-1])
                total = total + source[...].astype(F32)
        buf[own(0)] = total.astype(BF16)

    def far_first(self, axis):
        return sorted(range(1, self.size[axis]), key=lambda k: -min(k, self.size[axis] - k))

    def reduce_direct(self, buf, base, rows, axis, slots, spot):
        waits = []
        for k in self.far_first(axis):
            ticket = self.ticket()
            start = base + self.place(axis, k * self.turn) * rows
            slot = slots.at[pl.ds(spot + (k - 1) * rows, rows)]
            hops = min(k, self.size[axis] - k)
            self.copy(
                buf.at[pl.ds(start, rows)], slot, ticket,
                self.device(axis, k * self.turn), axis, hops,
            )
            waits.append((ticket, slot))
        here = pl.ds(base + self.at[axis] * rows, rows)
        total = buf[here].astype(F32)
        for ticket, slot in waits:
            yield ticket
            self.arrive(slot, ticket)
            total = total + slot[...].astype(F32)
        buf[here] = total.astype(BF16)

    def gather_direct(self, buf, base, rows, axis, arrived=None):
        def chunk(shift):
            start = base + self.place(axis, shift * self.turn) * rows
            return buf.at[pl.ds(start, rows)]

        waits = []
        for k in self.far_first(axis):
            ticket = self.ticket()
            hops = min(k, self.size[axis] - k)
            self.copy(
                chunk(0), chunk(0), ticket, self.device(axis, k * self.turn), axis, hops
            )
            waits.append((ticket, k))
        if arrived:
            arrived(0)
        for ticket, k in waits:
            yield ticket
            self.arrive(chunk(-k), ticket)
            if arrived:
                arrived(-k)

    def gather(self, buf, base, rows, axis, arrived=None):
        n = self.size[axis]
        if n == 1:
            if arrived:
                arrived(0)
            return
        lanes = [(1, n // 2), (-1, n // 2 - 1)]
        tickets = [[self.ticket() for _ in range(steps)] for _, steps in lanes]

        def chunk(shift):
            start = base + self.place(axis, shift) * rows
            return buf.at[pl.ds(start, rows)]

        def chain(lane, way, steps):
            for t in range(steps + 1):
                block = chunk(way * self.turn * t)
                if t > 0:
                    yield tickets[lane][t - 1]
                    self.arrive(block, tickets[lane][t - 1])
                if t < steps:
                    self.copy(
                        block, block, tickets[lane][t], self.device(axis, -way * self.turn), axis
                    )
                if t > 0 and arrived:
                    arrived(way * t)

        chains = [
            self.spawn(chain(lane, way, steps)) for lane, (way, steps) in enumerate(lanes) if steps
        ]
        if arrived:
            arrived(0)
        yield chains


def spread_out(rings, tab, base, total_rows, axes, forwards):
    mine = tab.at[rings.core]
    levels = []
    rows, start = total_rows, base
    for axis in axes:
        rows //= rings.size[axis]
        levels.append((axis, start, rows))
        start = start + rings.at[axis] * rows
    for depth in reversed(range(len(levels))):
        axis, first, rows = levels[depth]

        def forward(shift, axis=axis, first=first, rows=rows):
            ticket = rings.ticket()
            signed = shift * rings.turn
            here = pl.ds(first + rings.place(axis, signed) * rows, rows)
            there = pl.ds(first + rings.place(axis, -signed) * rows, rows)
            rings.copy(tab.at[rings.core, here], tab.at[rings.core, here], ticket, rings.sibling())
            forwards.append((tab.at[1 - rings.core, there], ticket))

        step = rings.gather_direct if depth or axis in DIRECT else rings.gather
        yield from step(mine, first, rows, axis, forward if depth == 0 else None)


def collect(rings, buf, base, total_rows, axes, slots, spot):
    rows, start = total_rows, base
    for depth, axis in enumerate(axes):
        rows //= rings.size[axis]
        step = rings.reduce_direct if depth or axis in DIRECT else rings.reduce
        yield from step(buf, start, rows, axis, slots, spot)
        spot += rows * (rings.size[axis] - 1)
        start = start + rings.at[axis] * rows


def chunk_start(rings, base, total_rows, axes):
    rows, start = total_rows, base
    for axis in axes:
        rows //= rings.size[axis]
        start = start + rings.at[axis] * rows
    return start, rows


ATOM_ORDERS = (("y", "x", "z"), ("z", "y", "x"), ("x", "y", "z"))


def atoms_stage(rings, index_s, mom_ref, other, green_ref, tab_ref, pot_ref, dense, slots):
    nz, nx, ny = (rings.size[a] for a in "zxy")
    held = nz * nx * ny
    part_rows = held

    def place(slot, order):
        spots = {"z": slot // (nx * ny), "x": lax.rem(slot // ny, nx), "y": lax.rem(slot, ny)}
        index = 0
        for axis in order:
            index = index * rings.size[axis] + spots[axis]
        return index

    def fill(slot, carry):
        value = mom_ref[index_s[0, slot]] + other[index_s[1, slot]]
        for part, order in enumerate(ATOM_ORDERS):
            dense[part * part_rows + place(slot, order)] = value[part * HALF_S : (part + 1) * HALF_S]
        return carry

    lax.fori_loop(0, held, fill, 0, unroll=4)
    forwards = []
    green = green_ref[...]
    column = lax.broadcasted_iota(jnp.int32, (DEG, HALF_S, L), 2) // DEG
    layer = lax.broadcasted_iota(jnp.int32, (DEG, HALF_S, L), 0)

    def task(part):
        order = ATOM_ORDERS[part]
        base = part * part_rows
        yield from collect(rings, dense, base, part_rows, order, slots, base)
        start, rows = chunk_start(rings, base, part_rows, order)
        charges = dense[start].astype(F32)
        stacked = jnp.concatenate([charges[:, :L], charges[:, L:]], axis=0).astype(BF16)
        result = jnp.dot(green, stacked, preferred_element_type=F32)
        sides = []
        for par in range(2):
            block = result[par * DEG * HALF_S : (par + 1) * DEG * HALF_S].reshape(DEG, HALF_S, L)
            sides.append(jnp.sum(jnp.where(column == layer, block, 0.0), axis=0))
        tab_ref[rings.core, start] = jnp.concatenate(sides, axis=1).astype(BF16)
        yield from spread_out(rings, tab_ref, base, part_rows, order, forwards)

    for part in range(3):
        rings.spawn(task(part))
    rings.run()
    for slot in range(ny):
        for part, order in enumerate(ATOM_ORDERS):
            index = 0
            for axis in order:
                index = index * rings.size[axis] + (slot if axis == "y" else rings.at[axis])
            pot_ref[slot, part * HALF_S : (part + 1) * HALF_S, :] = tab_ref[
                rings.core, part * part_rows + index
            ]
    for block, ticket in forwards:
        rings.arrive(block, ticket)


def field_stage(
    atoms_s, blocks_s, w_ref, phi_ref, tab_ref, out_ref, dist_ref, polar_ref, side_ref,
    acc_ref, operand_ref, pad_ref, mid_ref, inv_ref,
):
    count = dist_ref.shape[0] * 8
    basis, points = phi_ref.shape
    piece = basis // 2
    held = tab_ref.shape[1] // 3
    nx, planes = lax.axis_size("batch_1"), lax.axis_size("row") * lax.axis_size("col")
    sizes = {"z": lax.axis_size("batch_0"), "x": nx, "y": planes}
    wide = mid_ref.shape[1]
    row = lax.broadcasted_iota(jnp.int32, (S, wide), 0)
    shell = jnp.where(row < HALF_S, 2 * row, 2 * (row - HALF_S) + 1)
    acc_ref[...] = jnp.zeros_like(acc_ref)

    def eight(group, carry):
        for u in range(8):
            k = group * 8 + u
            atom = atoms_s[0, k]
            live = shell < 8 * blocks_s[atom]
            spots = {
                "z": lax.div(atom, nx * 2 * planes),
                "x": lax.rem(lax.div(atom, 2 * planes), nx),
                "y": lax.rem(atom, planes),
            }
            packed = []
            for part, order in enumerate(ATOM_ORDERS):
                index = 0
                for axis in order:
                    index = index * sizes[axis] + spots[axis]
                packed.append(tab_ref[lax.rem(lax.div(atom, planes), 2), part * held + index])
            packed = jnp.concatenate(packed, axis=0)
            table = jnp.concatenate([packed[:, :L], packed[:, L:]], axis=0)
            for first in range(0, points, wide):
                cols = slice(first, first + wide)
                ang = angular_of(polar_ref, side_ref, group, u, cols)
                spread = jnp.dot(table, ang, preferred_element_type=F32)
                rad = radial_of(dist_ref[group, u : u + 1, cols], mid_ref[...], inv_ref[...], live)
                for c in range(3):
                    total = acc_ref[c, :, cols]
                    for par in range(2):
                        row = par * 96 + c * HALF_S
                        prod = spread[row : row + HALF_S] * rad[par * HALF_S : (par + 1) * HALF_S]
                        for g in range(0, HALF_S, 8):
                            total = total + prod[g : g + 8]
                    acc_ref[c, :, cols] = total
        return carry

    lax.fori_loop(0, count // 8, eight, 0)
    for q in range(2):
        pad_ref[q, :piece, :] = phi_ref[q * piece : (q + 1) * piece, :]
        pad_ref[q, piece:, :] = jnp.zeros((128 - piece, points), BF16)
    for c in range(3):
        field = jnp.sum(acc_ref[c], axis=0, keepdims=True) * w_ref[...]
        for first in range(0, points, wide):
            cols = slice(first, first + wide)
            operand_ref[:, cols] = (phi_ref[:, cols].astype(F32) * field[:, cols]).astype(BF16)
        for q in range(2):
            local = lax.dot_general(
                operand_ref[...], pad_ref[q], NT, preferred_element_type=F32
            ).astype(BF16)
            for r in range(2):
                out_ref[r * 2 + q, :, c * 128 : (c + 1) * 128] = local[r * piece : (r + 1) * piece]


TILE_ORDERS = (("z", "x"), ("x", "z"))


def square_peers():
    n_row, n_col = lax.axis_size("row"), lax.axis_size("col")
    return [
        {
            "batch_2": lax.rem(lax.axis_index("batch_2") + dc, 2),
            "row": lax.rem(lax.axis_index("row") + dr, n_row),
            "col": lax.rem(lax.axis_index("col") + dl, n_col),
        }
        for dc in range(2)
        for dr in range(n_row)
        for dl in range(n_col)
        if dc or dr or dl
    ]


def matrix_stage(
    rings, quads_ref, label_ref, out_ref, tab_ref, flat, slots, got, marks, placed, hit
):
    row, col, core = (lax.axis_index(a) for a in ("row", "col", "batch_2"))
    n_row, n_col = lax.axis_size("row"), lax.axis_size("col")
    piece = quads_ref.shape[1]
    tile = hit.shape[0]
    half = tile // 2
    me = (core * n_row + row) * n_col + col
    waits = []
    for to in square_peers():
        first, second = rings.ticket(), rings.ticket()
        rings.copy(label_ref, marks.at[me], first, to)
        rings.copy(quads_ref.at[to["row"] * 2 + to["col"]], got.at[me], second, to)
        source = (to["batch_2"] * n_row + to["row"]) * n_col + to["col"]
        waits.append((marks.at[source], first, got.at[source], second))
    marks[me] = label_ref[...]
    got[me] = quads_ref[row * 2 + col]
    padded = flat.shape[0] - 3 * half * (tile // 128) // 16
    flat[flat.shape[0] - padded :] = jnp.zeros((padded, 16, 128), BF16)
    for mark, first, block, second in waits:
        rings.arrive(mark, first)
        rings.arrive(block, second)
    sources = 2 * n_row * n_col
    for s in range(sources):
        label = marks[s]
        rows_at = jnp.where(row == 0, label[0:1, :], label[1:2, :]) - row * tile - core * half
        cols_at = jnp.where(col == 0, label[0:1, :], label[1:2, :]) - col * tile
        row_hit = lax.broadcasted_iota(jnp.int32, (half, 128), 0) == rows_at
        row_hit = jnp.where(row_hit, 1.0, 0.0).astype(BF16)[:, :piece]
        spread = jnp.dot(row_hit, got[s], preferred_element_type=F32).astype(BF16)
        for c in range(3):
            placed[c * half : (c + 1) * half, s * 128 : (s + 1) * 128] = spread[
                :, c * 128 : (c + 1) * 128
            ]
        col_hit = lax.broadcasted_iota(jnp.int32, (tile, 128), 0) == cols_at
        hit[:, s * 128 : (s + 1) * 128] = jnp.where(col_hit, 1.0, 0.0).astype(BF16)
    groups = tile // 128
    for c in range(3):
        for j in range(tile // 256):
            block = lax.dot_general(
                placed[c * half : (c + 1) * half, :], hit[j * 256 : (j + 1) * 256, :], NT,
                preferred_element_type=F32,
            ).astype(BF16)
            for h in range(2):
                start = (c * groups + 2 * j + h) * half // 16
                flat[start : start + half // 16] = block[:, h * 128 : (h + 1) * 128].reshape(
                    half // 16, 16, 128
                )
    part_rows = flat.shape[0] // 2
    forwards = []

    def task(part):
        order = TILE_ORDERS[part]
        base = part * part_rows
        yield from collect(rings, flat, base, part_rows, order, slots, base)
        start, rows = chunk_start(rings, base, part_rows, order)
        here = pl.ds(start, rows)
        tab_ref[rings.core, here] = flat[here]
        yield from spread_out(rings, tab_ref, base, part_rows, order, forwards)

    for part in range(2):
        rings.spawn(task(part))
    rings.run()
    for block, ticket in forwards:
        rings.arrive(block, ticket)
    for h in range(2):
        for c in range(3):
            for g in range(groups):
                start = (c * groups + g) * half // 16
                out_ref[c, h * half : (h + 1) * half, g * 128 : (g + 1) * 128] = tab_ref[
                    h, start : start + half // 16
                ].reshape(half, 128)


def whole_kernel(
    index_s, atoms_s, blocks_s, atoms_ref, pos_ref, pts_ref, w_ref, widths_ref, phi_ref, dens_ref,
    green_ref, label_ref, pot_ref, out_ref,
    dist, polar, side, wd, scaled, ang, mid, inv, mom, other,
    dense, slots, tab, acc, operand, pad, quads, flat, slots_2, tab_2, got, marks, placed, hit,
    send, recv,
):
    rings = Rings(send, recv)
    met = [peer for peer in square_peers()]
    greeted = rings.greet("zx", met)
    moments_stage(
        atoms_s, blocks_s, atoms_ref, pos_ref, pts_ref, w_ref, widths_ref, phi_ref, dens_ref,
        mom, dist, polar, side, wd, scaled, ang, mid, inv,
    )
    pl.semaphore_wait(pltpu.get_barrier_semaphore(), greeted)
    ticket = rings.ticket()
    rings.copy(mom, other, ticket, rings.sibling())
    rings.arrive(other, ticket)
    atoms_stage(rings, index_s, mom, other, green_ref, tab, pot_ref, dense, slots)
    field_stage(
        atoms_s, blocks_s, w_ref, phi_ref, tab, quads, dist, polar, side, acc, operand, pad, mid, inv
    )
    matrix_stage(
        rings, quads, label_ref, out_ref, tab_2, flat, slots_2, got, marks, placed, hit
    )
    rings.finish()


def whole_call(index, atoms, blocks, pos, pts, w, widths, phi, dens, green, labels, sizes):
    count = atoms.shape[1]
    basis, points = phi.shape
    ring_devices, planes, tile = sizes
    held = ring_devices * planes
    half = tile // 2
    unit = 2 * 16 * ring_devices
    rows = -(-(3 * half * (tile // 128)) // unit) * unit
    sources = 2 * planes
    wide = min(256, points)
    return pl.pallas_call(
        whole_kernel,
        out_shape=(
            jax.ShapeDtypeStruct((planes, 96, 128), BF16),
            jax.ShapeDtypeStruct((3, tile, tile), BF16),
        ),
        in_specs=[smem()] * 3 + [vmem()] * 9,
        out_specs=(vmem(), vmem()),
        scratch_shapes=[
            pltpu.VMEM((count // 8, 8, points), F32),
            pltpu.VMEM((DEG, count // 8, 8, points), F32),
            pltpu.VMEM((DEG, count // 8, 8, points), F32),
            pltpu.VMEM((8, points), F32),
            pltpu.VMEM((2, 192, points), BF16),
            pltpu.VMEM((2, L, points), BF16),
            pltpu.VMEM((S, wide), F32),
            pltpu.VMEM((S, wide), F32),
            pltpu.VMEM((count + 1, 96, 128), BF16),
            pltpu.VMEM((count + 1, 96, 128), BF16),
            pltpu.VMEM((3 * held, HALF_S, 128), BF16),
            pltpu.VMEM((3 * held, HALF_S, 128), BF16),
            pltpu.VMEM((2, 3 * held, HALF_S, 128), BF16),
            pltpu.VMEM((3, 8, points), F32),
            pltpu.VMEM((basis, points), BF16),
            pltpu.VMEM((2, 128, points), BF16),
            pltpu.VMEM((4, basis // 2, 384), BF16),
            pltpu.VMEM((rows // 16, 16, 128), BF16),
            pltpu.VMEM((rows // 16, 16, 128), BF16),
            pltpu.VMEM((2, rows // 16, 16, 128), BF16),
            pltpu.VMEM((sources, basis // 2, 384), BF16),
            pltpu.VMEM((sources, 8, 128), jnp.int32),
            pltpu.VMEM((3 * half, sources * 128), BF16),
            pltpu.VMEM((tile, sources * 128), BF16),
            pltpu.SemaphoreType.DMA((192,)),
            pltpu.SemaphoreType.DMA((192,)),
        ],
        compiler_params=pltpu.CompilerParams(
            vmem_limit_bytes=VMEM_LIMIT, collective_id=0, has_side_effects=True
        ),
        name="whole",
    )(index, atoms, blocks, atoms, pos, pts, w, widths, phi, dens, green, labels)


def on_device(
    basis_values,
    density_matrix,
    points,
    weights,
    intersection,
    basis_index,
    atom_positions,
    shell_blocks,
    shell_widths,
    green,
):
    phi, dens, pts = basis_values[0], density_matrix[0], points[0]
    nz, nx = lax.axis_size("batch_0"), lax.axis_size("batch_1")
    n_row, n_col = lax.axis_size("row"), lax.axis_size("col")
    planes = n_row * n_col
    plane = lax.axis_index("col") * n_row + lax.axis_index("row")
    widths = shell_widths.reshape(1, S)

    count = intersection.shape[1]
    held = nz * nx * planes
    sibling_atoms = lax.ppermute(intersection, "batch_2", [(0, 1), (1, 0)])
    both = jnp.concatenate([intersection, sibling_atoms], axis=0)
    slot = jnp.arange(held)
    slot_atom = (slot // planes * 2 + lax.axis_index("batch_2")) * planes + slot % planes
    match = both[:, :, None] == slot_atom[None, None, :]
    index = count + jnp.sum(
        jnp.where(match, jnp.arange(count)[None, :, None] - count, 0), axis=1
    )
    mine = lax.dynamic_slice_in_dim(green, plane, 1, 0).reshape(DEG, HALF_S, 2, HALF_S, 2)
    mine = mine.transpose(2, 0, 1, 4, 3).reshape(2 * DEG * HALF_S, S)
    labels = jnp.pad(
        basis_index.reshape(2, -1), ((0, 6), (0, 128 - basis_index.shape[1] // 2)),
        constant_values=-(1 << 20),
    )
    tile = NB // n_row
    potential, matrix = whole_call(
        index, intersection, shell_blocks, atom_positions, pts, weights, widths, phi, dens, mine, labels,
        (nz * nx, planes, tile),
    )
    return potential.reshape(planes, -1), matrix


def solution(mesh):
    split = (8, 4, 2) if mesh.shape["batch"] == 64 else (mesh.shape["batch"] // 4, 2, 2)
    finer = Mesh(
        mesh.devices.reshape(*split, mesh.shape["row"], mesh.shape["col"]),
        BATCH_ROW_COL,
    )
    placed = (
        P(BATCH_ROW_COL, None, None),
        P(BATCH_ROW_COL, None, None, None),
        P(BATCH_ROW_COL, None, None),
        P(BATCH_ROW_COL, None),
        P(BATCH_ROW_COL, None),
        P(BATCH_ROW_COL, None),
        P(),
        P(),
        P(),
        P(BATCH, None, None),
    )
    return jax.shard_map(
        on_device,
        mesh=finer,
        in_specs=placed,
        out_specs=(P(BATCH, None), P(None, "row", "col")),
        check_vma=False,
    )
```

```python
import math

import jax
import jax.numpy as jnp
from jax import lax
from jax.experimental import pallas as pl
from jax.experimental.pallas import tpu as pltpu
from jax.sharding import Mesh
from jax.sharding import PartitionSpec as P

S = 64
DEG = 8
L = 64
NB = 1536
BATCH = ("batch_0", "batch_1", "batch_2")
BATCH_ROW_COL = ("batch_0", "batch_1", "batch_2", "row", "col")
MESH = pl.DeviceIdType.MESH
F32 = jnp.float32
BF16 = jnp.bfloat16
HALF_S = S // 2
RATE = {"z": 90e3, "x": 90e3, "y": 90e3, "core": 250e3}
HOP = 2.4
ISSUE = 0.08
DIRECT = ""
VMEM_LIMIT = 56 * 1024 * 1024
NT = (((1,), (1,)), ((), ()))


def vmem():
    return pl.BlockSpec(memory_space=pltpu.VMEM)


def smem():
    return pl.BlockSpec(memory_space=pltpu.SMEM)


def as_column(row):
    count = row.shape[1]
    down = lax.broadcasted_iota(jnp.int32, (count, count), 0)
    across = lax.broadcasted_iota(jnp.int32, (count, count), 1)
    return jnp.sum(jnp.where(down == across, row, 0), axis=1, keepdims=True)


def fill_rows(atoms_ref, pos_ref, pts_ref, dist_ref, polar_ref, side_ref):
    count = atoms_ref.shape[1]
    every = pos_ref.shape[1]
    picked = lax.broadcasted_iota(jnp.int32, (count, every), 1) == as_column(atoms_ref[...])
    centre = [
        jnp.sum(jnp.where(picked, pos_ref[d : d + 1, :], 0.0), axis=1, keepdims=True)
        for d in range(3)
    ]
    for group in range(count // 8):
        rows = slice(group * 8, group * 8 + 8)
        dx, dy, dz = [pts_ref[d] - centre[d][rows] for d in range(3)]
        dist = jnp.sqrt(dx * dx + dy * dy + dz * dz + 0.01)
        inverse = 1.0 / dist
        dist_ref[group] = dist
        for value, ref in ((dz * inverse, polar_ref), (dx * inverse, side_ref)):
            older, newer = jnp.ones_like(value), value
            ref[0, group] = older
            ref[1, group] = newer
            for order in range(2, DEG):
                older, newer = newer, 2.0 * value * newer - older
                ref[order, group] = newer


def shell_rows(widths_ref, lanes):
    row = lax.broadcasted_iota(jnp.int32, (S, lanes), 0)
    shell = jnp.where(row < HALF_S, 2 * row, 2 * (row - HALF_S) + 1)
    middle = shell.astype(F32) * (4.0 / S)
    row = lax.broadcasted_iota(jnp.int32, (S, S), 0)
    order = jnp.where(row < HALF_S, 2 * row, 2 * (row - HALF_S) + 1)
    picked = lax.broadcasted_iota(jnp.int32, (S, S), 1) == order
    widths = jnp.sum(jnp.where(picked, widths_ref[...], 0.0), axis=1, keepdims=True)
    scale = math.sqrt(math.log2(math.e)) / widths
    return shell, middle, jnp.broadcast_to(scale, (S, lanes))


def radial_of(dist, middle, scale, live):
    t = (dist - middle) * scale
    return jnp.where(live, jnp.exp2(-(t * t)), 0.0)


def angular_of(polar_ref, side_ref, group, u, cols):
    side = jnp.concatenate([side_ref[j, group, u : u + 1, cols] for j in range(DEG)], axis=0)
    return jnp.concatenate(
        [side * polar_ref[i, group, u : u + 1, cols] for i in range(DEG)], axis=0
    ).astype(BF16)


def moments_stage(
    atoms_s, blocks_s, atoms_ref, pos_ref, pts_ref, w_ref, widths_ref, phi_ref, dens_ref,
    out_ref, dist_ref, polar_ref, side_ref, wd_ref, scaled_ref, ang_ref, mid_ref, inv_ref,
):
    count = atoms_ref.shape[1]
    points = phi_ref.shape[1]
    fill_rows(atoms_ref, pos_ref, pts_ref, dist_ref, polar_ref, side_ref)
    wide = min(512, points)
    for first in range(0, points, wide):
        cols = slice(first, first + wide)
        phi = phi_ref[:, cols]
        for c in range(3):
            dphi = jnp.dot(dens_ref[c], phi, preferred_element_type=F32)
            total = jnp.sum(phi.astype(F32) * dphi, axis=0, keepdims=True)
            wd_ref[c : c + 1, cols] = total * w_ref[:, cols]
    shell, middle, scale = shell_rows(widths_ref, mid_ref.shape[1])
    shell = shell[:, :128]
    mid_ref[...] = middle
    inv_ref[...] = scale
    out_ref[count] = jnp.zeros((3 * HALF_S, 2 * L), BF16)

    def eight(group, carry):
        for u in range(8):
            k = group * 8 + u
            b = u % 2
            live = shell < 8 * blocks_s[atoms_s[0, k]]
            for first in range(0, points, 128):
                cols = slice(first, first + 128)
                rad = radial_of(
                    dist_ref[group, u : u + 1, cols], mid_ref[:, :128], inv_ref[:, :128], live
                )
                for c in range(3):
                    part = (rad * wd_ref[c : c + 1, cols]).astype(BF16)
                    for par in range(2):
                        row = par * 96 + c * HALF_S
                        scaled_ref[b, row : row + HALF_S, cols] = part[
                            par * HALF_S : (par + 1) * HALF_S
                        ]
                ang_ref[b, :, cols] = angular_of(polar_ref, side_ref, group, u, cols)
            got = lax.dot_general(scaled_ref[b], ang_ref[b], NT, preferred_element_type=F32)
            out_ref[k] = jnp.concatenate([got[:96], got[96:]], axis=1).astype(BF16)
        return carry

    lax.fori_loop(0, count // 8, eight, 0)


class Rings:
    def __init__(self, send, recv):
        self.send, self.recv = send, recv
        self.used = 0
        self.started = []
        self.now = 0.0
        self.free = {}
        self.lands = {}
        self.tasks = []
        self.core = lax.axis_index("batch_2")
        self.turn = 1 - 2 * self.core
        rows = lax.axis_size("row")
        self.size = {
            "z": lax.axis_size("batch_0"),
            "x": lax.axis_size("batch_1"),
            "y": rows * lax.axis_size("col"),
        }
        self.at = {
            "z": lax.axis_index("batch_0"),
            "x": lax.axis_index("batch_1"),
            "y": lax.axis_index("col") * rows + lax.axis_index("row"),
        }

    def place(self, axis, shift):
        n = self.size[axis]
        return lax.rem(self.at[axis] + shift + 2 * n, n)

    def device(self, axis, shift):
        spot = self.place(axis, shift)
        if axis == "z":
            return {"batch_0": spot}
        if axis == "x":
            return {"batch_1": spot}
        rows = lax.axis_size("row")
        return {"row": lax.rem(spot, rows), "col": spot // rows}

    def sibling(self):
        return {"batch_2": 1 - self.core}

    def greet(self, axes, others=()):
        barrier = pltpu.get_barrier_semaphore()
        greeted = 0
        for axis in axes:
            for shift in range(1, self.size[axis]):
                pl.semaphore_signal(
                    barrier, inc=1, device_id=self.device(axis, shift), device_id_type=MESH
                )
                greeted += 1
        for other in others:
            pl.semaphore_signal(barrier, inc=1, device_id=other, device_id_type=MESH)
            greeted += 1
        return greeted

    def ticket(self):
        self.used += 1
        return self.used - 1

    def copy(self, src, dst, ticket, device, link="core", hops=1):
        made = pltpu.make_async_remote_copy(
            src_ref=src, dst_ref=dst, send_sem=self.send.at[ticket],
            recv_sem=self.recv.at[ticket], device_id=device, device_id_type=MESH,
        )
        made.start()
        self.started.append(made)
        took = hops * math.prod(src.shape) * 2 / RATE[link]
        self.free[link] = max(self.free.get(link, 0.0), self.now) + took
        self.lands[ticket] = self.free[link] + HOP
        self.now += ISSUE

    def spawn(self, work):
        task = [work, None]
        self.tasks.append(task)
        self.step(task)
        return task

    def step(self, task):
        try:
            task[1] = next(task[0])
        except StopIteration:
            self.tasks.remove(task)

    def ready(self, task):
        wanted = task[1]
        if isinstance(wanted, list):
            return math.inf if any(other in self.tasks for other in wanted) else self.now
        return self.lands.get(wanted, math.inf)

    def run(self):
        while self.tasks:
            task = min(self.tasks, key=self.ready)
            self.now = max(self.now, self.ready(task)) + ISSUE
            self.step(task)

    def arrive(self, dst, ticket):
        pltpu.make_async_remote_copy(
            src_ref=dst, dst_ref=dst, send_sem=self.send.at[ticket],
            recv_sem=self.recv.at[ticket], device_id=self.sibling(), device_id_type=MESH,
        ).wait_recv()

    def finish(self):
        for made in self.started:
            made.wait_send()

    def reduce(self, buf, base, rows, axis, slots, spot):
        n = self.size[axis]
        if n == 1:
            return
        lanes = [(1, n // 2), (-1, n // 2 - 1)]
        subs = 2 if rows % 2 == 0 else 1
        per = rows // subs
        tickets, places = {}, {}
        for sub in range(subs):
            for lane, (_, steps) in enumerate(lanes):
                tickets[lane, sub] = [self.ticket() for _ in range(steps)]
                places[lane, sub] = [spot + per * k for k in range(steps)]
                spot += per * steps

        def own(shift, sub):
            return pl.ds(base + self.place(axis, shift) * rows + sub * per, per)

        def chain(lane, sub, way, steps):
            ticket, spots = tickets[lane, sub], places[lane, sub]
            for t in range(steps):
                mine = own(-way * self.turn * (steps - t), sub)
                if t == 0:
                    source = buf.at[mine]
                else:
                    source = slots.at[pl.ds(spots[t - 1], per)]
                    yield ticket[t - 1]
                    self.arrive(source, ticket[t - 1])
                    source[...] = (source[...].astype(F32) + buf[mine].astype(F32)).astype(BF16)
                self.copy(
                    source, slots.at[pl.ds(spots[t], per)], ticket[t],
                    self.device(axis, -way * self.turn), axis,
                )

        for sub in range(subs):
            for lane, (way, steps) in enumerate(lanes):
                if steps:
                    self.spawn(chain(lane, sub, way, steps))
        for sub in range(subs):
            total = buf[own(0, sub)].astype(F32)
            for lane, (way, steps) in enumerate(lanes):
                if steps:
                    source = slots.at[pl.ds(places[lane, sub][-1], per)]
                    yield tickets[lane, sub][-1]
                    self.arrive(source, tickets[lane, sub][-1])
                    total = total + source[...].astype(F32)
            buf[own(0, sub)] = total.astype(BF16)

    def far_first(self, axis):
        return sorted(range(1, self.size[axis]), key=lambda k: -min(k, self.size[axis] - k))

    def reduce_direct(self, buf, base, rows, axis, slots, spot):
        waits = []
        for k in self.far_first(axis):
            ticket = self.ticket()
            start = base + self.place(axis, k * self.turn) * rows
            slot = slots.at[pl.ds(spot + (k - 1) * rows, rows)]
            hops = min(k, self.size[axis] - k)
            self.copy(
                buf.at[pl.ds(start, rows)], slot, ticket,
                self.device(axis, k * self.turn), axis, hops,
            )
            waits.append((ticket, slot))
        here = pl.ds(base + self.at[axis] * rows, rows)
        total = buf[here].astype(F32)
        for ticket, slot in waits:
            yield ticket
            self.arrive(slot, ticket)
            total = total + slot[...].astype(F32)
        buf[here] = total.astype(BF16)

    def gather_direct(self, buf, base, rows, axis, arrived=None):
        def chunk(shift):
            start = base + self.place(axis, shift * self.turn) * rows
            return buf.at[pl.ds(start, rows)]

        waits = []
        for k in self.far_first(axis):
            ticket = self.ticket()
            hops = min(k, self.size[axis] - k)
            self.copy(
                chunk(0), chunk(0), ticket, self.device(axis, k * self.turn), axis, hops
            )
            waits.append((ticket, k))
        if arrived:
            arrived(0)
        for ticket, k in waits:
            yield ticket
            self.arrive(chunk(-k), ticket)
            if arrived:
                arrived(-k)

    def gather(self, buf, base, rows, axis, arrived=None):
        n = self.size[axis]
        if n == 1:
            if arrived:
                arrived(0)
            return
        lanes = [(1, n // 2), (-1, n // 2 - 1)]
        subs = 2 if rows % 2 == 0 else 1
        per = rows // subs
        tickets = {}
        for sub in range(subs):
            for lane, (_, steps) in enumerate(lanes):
                tickets[lane, sub] = [self.ticket() for _ in range(steps)]

        def chunk(shift, sub):
            return buf.at[pl.ds(base + self.place(axis, shift) * rows + sub * per, per)]

        def chain(lane, sub, way, steps):
            ticket = tickets[lane, sub]
            for t in range(steps + 1):
                block = chunk(way * self.turn * t, sub)
                if t > 0:
                    yield ticket[t - 1]
                    self.arrive(block, ticket[t - 1])
                if t < steps:
                    self.copy(block, block, ticket[t], self.device(axis, -way * self.turn), axis)
                if t > 0 and arrived:
                    arrived(way * t, sub, subs)

        chains = [
            self.spawn(chain(lane, sub, way, steps))
            for sub in range(subs)
            for lane, (way, steps) in enumerate(lanes)
            if steps
        ]
        if arrived:
            arrived(0)
        yield chains


def spread_out(rings, tab, base, total_rows, axes, forwards):
    mine = tab.at[rings.core]
    levels = []
    rows, start = total_rows, base
    for axis in axes:
        rows //= rings.size[axis]
        levels.append((axis, start, rows))
        start = start + rings.at[axis] * rows
    for depth in reversed(range(len(levels))):
        axis, first, rows = levels[depth]

        def forward(shift, sub=0, subs=1, axis=axis, first=first, rows=rows):
            ticket = rings.ticket()
            signed = shift * rings.turn
            per = rows // subs
            here = pl.ds(first + rings.place(axis, signed) * rows + sub * per, per)
            there = pl.ds(first + rings.place(axis, -signed) * rows + sub * per, per)
            rings.copy(tab.at[rings.core, here], tab.at[rings.core, here], ticket, rings.sibling())
            forwards.append((tab.at[1 - rings.core, there], ticket))

        step = rings.gather_direct if depth or axis in DIRECT else rings.gather
        yield from step(mine, first, rows, axis, forward if depth == 0 else None)


def collect(rings, buf, base, total_rows, axes, slots, spot):
    rows, start = total_rows, base
    for depth, axis in enumerate(axes):
        rows //= rings.size[axis]
        step = rings.reduce_direct if depth or axis in DIRECT else rings.reduce
        yield from step(buf, start, rows, axis, slots, spot)
        spot += rows * (rings.size[axis] - 1)
        start = start + rings.at[axis] * rows


def chunk_start(rings, base, total_rows, axes):
    rows, start = total_rows, base
    for axis in axes:
        rows //= rings.size[axis]
        start = start + rings.at[axis] * rows
    return start, rows


ATOM_ORDERS = (("y", "x", "z"), ("z", "y", "x"), ("x", "y", "z"))


def atoms_stage(rings, index_s, mom_ref, other, green_ref, tab_ref, pot_ref, dense, slots):
    nz, nx, ny = (rings.size[a] for a in "zxy")
    held = nz * nx * ny
    part_rows = held

    def place(slot, order):
        spots = {"z": slot // (nx * ny), "x": lax.rem(slot // ny, nx), "y": lax.rem(slot, ny)}
        index = 0
        for axis in order:
            index = index * rings.size[axis] + spots[axis]
        return index

    def fill(slot, carry):
        value = mom_ref[index_s[0, slot]] + other[index_s[1, slot]]
        for part, order in enumerate(ATOM_ORDERS):
            dense[part * part_rows + place(slot, order)] = value[part * HALF_S : (part + 1) * HALF_S]
        return carry

    lax.fori_loop(0, held, fill, 0, unroll=4)
    forwards = []
    green = green_ref[...]
    column = lax.broadcasted_iota(jnp.int32, (DEG, HALF_S, L), 2) // DEG
    layer = lax.broadcasted_iota(jnp.int32, (DEG, HALF_S, L), 0)

    def task(part):
        order = ATOM_ORDERS[part]
        base = part * part_rows
        yield from collect(rings, dense, base, part_rows, order, slots, base)
        start, rows = chunk_start(rings, base, part_rows, order)
        charges = dense[start].astype(F32)
        stacked = jnp.concatenate([charges[:, :L], charges[:, L:]], axis=0).astype(BF16)
        result = jnp.dot(green, stacked, preferred_element_type=F32)
        sides = []
        for par in range(2):
            block = result[par * DEG * HALF_S : (par + 1) * DEG * HALF_S].reshape(DEG, HALF_S, L)
            sides.append(jnp.sum(jnp.where(column == layer, block, 0.0), axis=0))
        tab_ref[rings.core, start] = jnp.concatenate(sides, axis=1).astype(BF16)
        yield from spread_out(rings, tab_ref, base, part_rows, order, forwards)

    for part in range(3):
        rings.spawn(task(part))
    rings.run()
    for slot in range(ny):
        for part, order in enumerate(ATOM_ORDERS):
            index = 0
            for axis in order:
                index = index * rings.size[axis] + (slot if axis == "y" else rings.at[axis])
            pot_ref[slot, part * HALF_S : (part + 1) * HALF_S, :] = tab_ref[
                rings.core, part * part_rows + index
            ]
    for block, ticket in forwards:
        rings.arrive(block, ticket)


def field_stage(
    atoms_s, blocks_s, w_ref, phi_ref, tab_ref, out_ref, dist_ref, polar_ref, side_ref,
    acc_ref, operand_ref, pad_ref, mid_ref, inv_ref,
):
    count = dist_ref.shape[0] * 8
    basis, points = phi_ref.shape
    piece = basis // 2
    held = tab_ref.shape[1] // 3
    nx, planes = lax.axis_size("batch_1"), lax.axis_size("row") * lax.axis_size("col")
    sizes = {"z": lax.axis_size("batch_0"), "x": nx, "y": planes}
    wide = mid_ref.shape[1]
    row = lax.broadcasted_iota(jnp.int32, (S, wide), 0)
    shell = jnp.where(row < HALF_S, 2 * row, 2 * (row - HALF_S) + 1)
    acc_ref[...] = jnp.zeros_like(acc_ref)

    def eight(group, carry):
        for u in range(8):
            k = group * 8 + u
            atom = atoms_s[0, k]
            live = shell < 8 * blocks_s[atom]
            spots = {
                "z": lax.div(atom, nx * 2 * planes),
                "x": lax.rem(lax.div(atom, 2 * planes), nx),
                "y": lax.rem(atom, planes),
            }
            packed = []
            for part, order in enumerate(ATOM_ORDERS):
                index = 0
                for axis in order:
                    index = index * sizes[axis] + spots[axis]
                packed.append(tab_ref[lax.rem(lax.div(atom, planes), 2), part * held + index])
            packed = jnp.concatenate(packed, axis=0)
            table = jnp.concatenate([packed[:, :L], packed[:, L:]], axis=0)
            for first in range(0, points, wide):
                cols = slice(first, first + wide)
                ang = angular_of(polar_ref, side_ref, group, u, cols)
                spread = jnp.dot(table, ang, preferred_element_type=F32)
                rad = radial_of(dist_ref[group, u : u + 1, cols], mid_ref[...], inv_ref[...], live)
                for c in range(3):
                    total = acc_ref[c, :, cols]
                    for par in range(2):
                        row = par * 96 + c * HALF_S
                        prod = spread[row : row + HALF_S] * rad[par * HALF_S : (par + 1) * HALF_S]
                        for g in range(0, HALF_S, 8):
                            total = total + prod[g : g + 8]
                    acc_ref[c, :, cols] = total
        return carry

    lax.fori_loop(0, count // 8, eight, 0)
    for q in range(2):
        pad_ref[q, :piece, :] = phi_ref[q * piece : (q + 1) * piece, :]
        pad_ref[q, piece:, :] = jnp.zeros((128 - piece, points), BF16)
    for c in range(3):
        field = jnp.sum(acc_ref[c], axis=0, keepdims=True) * w_ref[...]
        for first in range(0, points, wide):
            cols = slice(first, first + wide)
            operand_ref[:, cols] = (phi_ref[:, cols].astype(F32) * field[:, cols]).astype(BF16)
        for q in range(2):
            local = lax.dot_general(
                operand_ref[...], pad_ref[q], NT, preferred_element_type=F32
            ).astype(BF16)
            for r in range(2):
                out_ref[r * 2 + q, c] = local[r * piece : (r + 1) * piece]


TILE_ORDERS = (("z", "x"), ("x", "z"))


def square_peers():
    n_row, n_col = lax.axis_size("row"), lax.axis_size("col")
    return [
        {
            "batch_2": lax.rem(lax.axis_index("batch_2") + dc, 2),
            "row": lax.rem(lax.axis_index("row") + dr, n_row),
            "col": lax.rem(lax.axis_index("col") + dl, n_col),
        }
        for dc in range(2)
        for dr in range(n_row)
        for dl in range(n_col)
        if dc or dr or dl
    ]


def matrix_stage(
    rings, quads_ref, label_ref, out_ref, tab_ref, flat, slots, got, marks, placed, hit
):
    row, col, core = (lax.axis_index(a) for a in ("row", "col", "batch_2"))
    n_row, n_col = lax.axis_size("row"), lax.axis_size("col")
    piece = quads_ref.shape[2]
    tile = hit.shape[0]
    half = tile // 2
    me = (core * n_row + row) * n_col + col
    waits = []
    for to in square_peers():
        first, second = rings.ticket(), rings.ticket()
        rings.copy(label_ref, marks.at[me], first, to)
        wanted = quads_ref.at[to["row"] * 2 + to["col"], pl.ds(to["batch_2"], 2)]
        rings.copy(wanted, got.at[me], second, to)
        source = (to["batch_2"] * n_row + to["row"]) * n_col + to["col"]
        waits.append((marks.at[source], first, got.at[source], second))
    marks[me] = label_ref[...]
    got[me] = quads_ref[row * 2 + col, pl.ds(core, 2)]
    padded = flat.shape[0] - 3 * half * (tile // 128) // 16
    flat[flat.shape[0] - padded :] = jnp.zeros((padded, 16, 128), BF16)
    for mark, first, block, second in waits:
        rings.arrive(mark, first)
        rings.arrive(block, second)
    sources = 2 * n_row * n_col
    for s in range(sources):
        label = marks[s]
        rows_at = jnp.where(row == 0, label[0:1, :], label[1:2, :]) - row * tile
        cols_at = jnp.where(col == 0, label[0:1, :], label[1:2, :]) - col * tile
        for first, count, shift, which in ((0, tile, 0, core), (tile, half, core * half, 1 - core)):
            row_hit = lax.broadcasted_iota(jnp.int32, (count, 128), 0) == rows_at - shift
            row_hit = jnp.where(row_hit, 1.0, 0.0).astype(BF16)[:, :piece]
            spread = jnp.dot(row_hit, got[s, which], preferred_element_type=F32).astype(BF16)
            placed[first : first + count, s * 128 : (s + 1) * 128] = spread
        col_hit = lax.broadcasted_iota(jnp.int32, (tile, 128), 0) == cols_at
        hit[:, s * 128 : (s + 1) * 128] = jnp.where(col_hit, 1.0, 0.0).astype(BF16)
    groups = tile // 128
    for c in range(3):
        for j in range(tile // 256):
            block = lax.dot_general(
                placed[c * half : (c + 1) * half, :], hit[j * 256 : (j + 1) * 256, :], NT,
                preferred_element_type=F32,
            ).astype(BF16)
            for h in range(2):
                start = (c * groups + 2 * j + h) * half // 16
                flat[start : start + half // 16] = block[:, h * 128 : (h + 1) * 128].reshape(
                    half // 16, 16, 128
                )
    part_rows = flat.shape[0] // 2
    forwards = []

    def task(part):
        order = TILE_ORDERS[part]
        base = part * part_rows
        yield from collect(rings, flat, base, part_rows, order, slots, base)
        start, rows = chunk_start(rings, base, part_rows, order)
        here = pl.ds(start, rows)
        tab_ref[rings.core, here] = flat[here]
        yield from spread_out(rings, tab_ref, base, part_rows, order, forwards)

    for part in range(2):
        rings.spawn(task(part))
    rings.run()
    for block, ticket in forwards:
        rings.arrive(block, ticket)
    for h in range(2):
        for c, (comp, first) in enumerate(((2 * h, 0), (2 * h, half), (1, h * half))):
            for g in range(groups):
                start = (c * groups + g) * half // 16
                out_ref[comp, first : first + half, g * 128 : (g + 1) * 128] = tab_ref[
                    h, start : start + half // 16
                ].reshape(half, 128)


def whole_kernel(
    index_s, atoms_s, blocks_s, atoms_ref, pos_ref, pts_ref, w_ref, widths_ref, phi_ref, dens_ref,
    green_ref, basis_ref, pot_ref, out_ref,
    dist, polar, side, wd, scaled, ang, mid, inv, mom, other,
    dense, slots, tab, acc, operand, pad, quads, flat, slots_2, tab_2, got, marks, placed, hit,
    label, send, recv,
):
    rings = Rings(send, recv)
    met = [peer for peer in square_peers()]
    greeted = rings.greet("zx", met)
    none = jnp.full((8, 128), -(1 << 20), jnp.int32)
    label[...] = none
    piece = basis_ref.shape[1] // 2
    for q in range(2):
        part = basis_ref[:, q * piece : (q + 1) * piece]
        label[q : q + 1, :] = jnp.concatenate([part, none[:1, piece:]], axis=1)
    moments_stage(
        atoms_s, blocks_s, atoms_ref, pos_ref, pts_ref, w_ref, widths_ref, phi_ref, dens_ref,
        mom, dist, polar, side, wd, scaled, ang, mid, inv,
    )
    pl.semaphore_wait(pltpu.get_barrier_semaphore(), greeted)
    ticket = rings.ticket()
    rings.copy(mom, other, ticket, rings.sibling())
    rings.arrive(other, ticket)
    atoms_stage(rings, index_s, mom, other, green_ref, tab, pot_ref, dense, slots)
    field_stage(
        atoms_s, blocks_s, w_ref, phi_ref, tab, quads, dist, polar, side, acc, operand, pad, mid, inv
    )
    matrix_stage(
        rings, quads, label, out_ref, tab_2, flat, slots_2, got, marks, placed, hit
    )
    rings.finish()


def whole_call(index, atoms, blocks, pos, pts, w, widths, phi, dens, green, labels, sizes):
    count = atoms.shape[1]
    basis, points = phi.shape
    ring_devices, planes, tile = sizes
    held = ring_devices * planes
    half = tile // 2
    unit = 2 * 16 * ring_devices
    rows = -(-(3 * half * (tile // 128)) // unit) * unit
    sources = 2 * planes
    wide = min(256, points)
    return pl.pallas_call(
        whole_kernel,
        out_shape=(
            jax.ShapeDtypeStruct((planes, 96, 128), BF16),
            jax.ShapeDtypeStruct((3, tile, tile), BF16),
        ),
        in_specs=[smem()] * 3 + [vmem()] * 9,
        out_specs=(vmem(), vmem()),
        scratch_shapes=[
            pltpu.VMEM((count // 8, 8, points), F32),
            pltpu.VMEM((DEG, count // 8, 8, points), F32),
            pltpu.VMEM((DEG, count // 8, 8, points), F32),
            pltpu.VMEM((8, points), F32),
            pltpu.VMEM((2, 192, points), BF16),
            pltpu.VMEM((2, L, points), BF16),
            pltpu.VMEM((S, wide), F32),
            pltpu.VMEM((S, wide), F32),
            pltpu.VMEM((count + 1, 96, 128), BF16),
            pltpu.VMEM((count + 1, 96, 128), BF16),
            pltpu.VMEM((3 * held, HALF_S, 128), BF16),
            pltpu.VMEM((3 * held, HALF_S, 128), BF16),
            pltpu.VMEM((2, 3 * held, HALF_S, 128), BF16),
            pltpu.VMEM((3, 8, points), F32),
            pltpu.VMEM((basis, points), BF16),
            pltpu.VMEM((2, 128, points), BF16),
            pltpu.VMEM((4, 3, basis // 2, 128), BF16),
            pltpu.VMEM((rows // 16, 16, 128), BF16),
            pltpu.VMEM((rows // 16, 16, 128), BF16),
            pltpu.VMEM((2, rows // 16, 16, 128), BF16),
            pltpu.VMEM((sources, 2, basis // 2, 128), BF16),
            pltpu.VMEM((sources, 8, 128), jnp.int32),
            pltpu.VMEM((3 * half, sources * 128), BF16),
            pltpu.VMEM((tile, sources * 128), BF16),
            pltpu.VMEM((8, 128), jnp.int32),
            pltpu.SemaphoreType.DMA((256,)),
            pltpu.SemaphoreType.DMA((256,)),
        ],
        compiler_params=pltpu.CompilerParams(
            vmem_limit_bytes=VMEM_LIMIT, collective_id=0, has_side_effects=True
        ),
        name="whole",
    )(index, atoms, blocks, atoms, pos, pts, w, widths, phi, dens, green, labels)


def on_device(
    basis_values,
    density_matrix,
    points,
    weights,
    intersection,
    basis_index,
    atom_positions,
    shell_blocks,
    shell_widths,
    green,
):
    phi, dens, pts = basis_values[0], density_matrix[0], points.transpose(1, 0, 2)
    nz, nx = lax.axis_size("batch_0"), lax.axis_size("batch_1")
    n_row, n_col = lax.axis_size("row"), lax.axis_size("col")
    planes = n_row * n_col
    plane = lax.axis_index("col") * n_row + lax.axis_index("row")
    widths = shell_widths.reshape(1, S)

    count = intersection.shape[1]
    held = nz * nx * planes
    sibling_atoms = lax.ppermute(intersection, "batch_2", [(0, 1), (1, 0)])
    both = jnp.concatenate([intersection, sibling_atoms], axis=0)
    slot = jnp.arange(held)
    slot_atom = (slot // planes * 2 + lax.axis_index("batch_2")) * planes + slot % planes
    match = both[:, :, None] == slot_atom[None, None, :]
    index = count + jnp.sum(
        jnp.where(match, jnp.arange(count)[None, :, None] - count, 0), axis=1
    )
    mine = lax.dynamic_slice_in_dim(green, plane, 1, 0).reshape(DEG, HALF_S, 2, HALF_S, 2)
    mine = mine.transpose(2, 0, 1, 4, 3).reshape(2 * DEG * HALF_S, S)
    tile = NB // n_row
    potential, matrix = whole_call(
        index, intersection, shell_blocks, atom_positions, pts, weights, widths, phi, dens, mine, basis_index,
        (nz * nx, planes, tile),
    )
    return potential.reshape(planes, -1), matrix


def solution(mesh):
    split = (8, 4, 2) if mesh.shape["batch"] == 64 else (mesh.shape["batch"] // 4, 2, 2)
    finer = Mesh(
        mesh.devices.reshape(*split, mesh.shape["row"], mesh.shape["col"]),
        BATCH_ROW_COL,
    )
    placed = (
        P(BATCH_ROW_COL, None, None),
        P(BATCH_ROW_COL, None, None, None),
        P(BATCH_ROW_COL, None, None),
        P(BATCH_ROW_COL, None),
        P(BATCH_ROW_COL, None),
        P(BATCH_ROW_COL, None),
        P(),
        P(),
        P(),
        P(BATCH, None, None),
    )
    return jax.shard_map(
        on_device,
        mesh=finer,
        in_specs=placed,
        out_specs=(P(BATCH, None), P(None, "row", "col")),
        check_vma=False,
    )
```

```python
import math

import jax
import jax.numpy as jnp
from jax import lax
from jax.experimental import pallas as pl
from jax.experimental.pallas import tpu as pltpu
from jax.sharding import Mesh
from jax.sharding import PartitionSpec as P

S = 64
DEG = 8
L = 64
NB = 1536
BATCH = ("batch_0", "batch_1", "batch_2")
BATCH_ROW_COL = ("batch_0", "batch_1", "batch_2", "row", "col")
MESH = pl.DeviceIdType.MESH
F32 = jnp.float32
BF16 = jnp.bfloat16
HALF_S = S // 2
RATE = {"z": 90e3, "x": 90e3, "y": 90e3, "core": 250e3}
HOP = 2.4
ISSUE = 0.08
DIRECT = ""
VMEM_LIMIT = 56 * 1024 * 1024
NT = (((1,), (1,)), ((), ()))


def vmem():
    return pl.BlockSpec(memory_space=pltpu.VMEM)


def smem():
    return pl.BlockSpec(memory_space=pltpu.SMEM)


def as_column(row):
    count = row.shape[1]
    down = lax.broadcasted_iota(jnp.int32, (count, count), 0)
    across = lax.broadcasted_iota(jnp.int32, (count, count), 1)
    return jnp.sum(jnp.where(down == across, row, 0), axis=1, keepdims=True)


def fill_rows(atoms_ref, pos_ref, pts_ref, dist_ref, polar_ref, side_ref):
    count = atoms_ref.shape[1]
    every = pos_ref.shape[1]
    picked = lax.broadcasted_iota(jnp.int32, (count, every), 1) == as_column(atoms_ref[...])
    centre = [
        jnp.sum(jnp.where(picked, pos_ref[d : d + 1, :], 0.0), axis=1, keepdims=True)
        for d in range(3)
    ]
    for group in range(count // 8):
        rows = slice(group * 8, group * 8 + 8)
        dx, dy, dz = [pts_ref[d] - centre[d][rows] for d in range(3)]
        dist = jnp.sqrt(dx * dx + dy * dy + dz * dz + 0.01)
        inverse = 1.0 / dist
        dist_ref[group] = dist
        for value, ref in ((dz * inverse, polar_ref), (dx * inverse, side_ref)):
            older, newer = jnp.ones_like(value), value
            ref[0, group] = older
            ref[1, group] = newer
            for order in range(2, DEG):
                older, newer = newer, 2.0 * value * newer - older
                ref[order, group] = newer


def shell_rows(widths_ref, lanes):
    row = lax.broadcasted_iota(jnp.int32, (S, lanes), 0)
    shell = jnp.where(row < HALF_S, 2 * row, 2 * (row - HALF_S) + 1)
    middle = shell.astype(F32) * (4.0 / S)
    row = lax.broadcasted_iota(jnp.int32, (S, S), 0)
    order = jnp.where(row < HALF_S, 2 * row, 2 * (row - HALF_S) + 1)
    picked = lax.broadcasted_iota(jnp.int32, (S, S), 1) == order
    widths = jnp.sum(jnp.where(picked, widths_ref[...], 0.0), axis=1, keepdims=True)
    scale = math.sqrt(math.log2(math.e)) / widths
    return shell, middle, jnp.broadcast_to(scale, (S, lanes))


def radial_of(dist, middle, scale, live):
    t = (dist - middle) * scale
    return jnp.where(live, jnp.exp2(-(t * t)), 0.0)


def angular_of(polar_ref, side_ref, group, u, cols):
    side = jnp.concatenate([side_ref[j, group, u : u + 1, cols] for j in range(DEG)], axis=0)
    return jnp.concatenate(
        [side * polar_ref[i, group, u : u + 1, cols] for i in range(DEG)], axis=0
    ).astype(BF16)


def moments_stage(
    atoms_s, blocks_s, atoms_ref, pos_ref, pts_ref, w_ref, widths_ref, phi_ref, dens_ref,
    out_ref, dist_ref, polar_ref, side_ref, wd_ref, scaled_ref, ang_ref, mid_ref, inv_ref,
    between,
):
    count = atoms_ref.shape[1]
    points = phi_ref.shape[1]
    fill_rows(atoms_ref, pos_ref, pts_ref, dist_ref, polar_ref, side_ref)
    wide = min(512, points)
    for first in range(0, points, wide):
        cols = slice(first, first + wide)
        phi = phi_ref[:, cols]
        for c in range(3):
            dphi = jnp.dot(dens_ref[c], phi, preferred_element_type=F32)
            total = jnp.sum(phi.astype(F32) * dphi, axis=0, keepdims=True)
            wd_ref[c : c + 1, cols] = total * w_ref[:, cols]
    shell, middle, scale = shell_rows(widths_ref, mid_ref.shape[1])
    shell = shell[:, :128]
    mid_ref[...] = middle
    inv_ref[...] = scale
    out_ref[count] = jnp.zeros((3 * HALF_S, 2 * L), BF16)

    def eight(group, carry):
        for u in range(8):
            k = group * 8 + u
            b = u % 2
            live = shell < 8 * blocks_s[atoms_s[0, k]]
            for first in range(0, points, 128):
                cols = slice(first, first + 128)
                rad = radial_of(
                    dist_ref[group, u : u + 1, cols], mid_ref[:, :128], inv_ref[:, :128], live
                )
                for c in range(3):
                    part = (rad * wd_ref[c : c + 1, cols]).astype(BF16)
                    for par in range(2):
                        row = par * 96 + c * HALF_S
                        scaled_ref[b, row : row + HALF_S, cols] = part[
                            par * HALF_S : (par + 1) * HALF_S
                        ]
                ang_ref[b, :, cols] = angular_of(polar_ref, side_ref, group, u, cols)
            got = lax.dot_general(scaled_ref[b], ang_ref[b], NT, preferred_element_type=F32)
            out_ref[k] = jnp.concatenate([got[:96], got[96:]], axis=1).astype(BF16)
        return carry

    groups = count // 8
    lax.fori_loop(0, groups // 2, eight, 0)
    between()
    lax.fori_loop(groups // 2, groups, eight, 0)


class Rings:
    def __init__(self, send, recv):
        self.send, self.recv = send, recv
        self.used = 0
        self.started = []
        self.now = 0.0
        self.free = {}
        self.lands = {}
        self.tasks = []
        self.core = lax.axis_index("batch_2")
        self.turn = 1 - 2 * self.core
        rows = lax.axis_size("row")
        self.size = {
            "z": lax.axis_size("batch_0"),
            "x": lax.axis_size("batch_1"),
            "y": rows * lax.axis_size("col"),
        }
        self.at = {
            "z": lax.axis_index("batch_0"),
            "x": lax.axis_index("batch_1"),
            "y": lax.axis_index("col") * rows + lax.axis_index("row"),
        }

    def place(self, axis, shift):
        n = self.size[axis]
        return lax.rem(self.at[axis] + shift + 2 * n, n)

    def device(self, axis, shift):
        spot = self.place(axis, shift)
        if axis == "z":
            return {"batch_0": spot}
        if axis == "x":
            return {"batch_1": spot}
        rows = lax.axis_size("row")
        return {"row": lax.rem(spot, rows), "col": spot // rows}

    def sibling(self):
        return {"batch_2": 1 - self.core}

    def greet(self, axes, others=()):
        barrier = pltpu.get_barrier_semaphore()
        greeted = 0
        for axis in axes:
            for shift in range(1, self.size[axis]):
                pl.semaphore_signal(
                    barrier, inc=1, device_id=self.device(axis, shift), device_id_type=MESH
                )
                greeted += 1
        for other in others:
            pl.semaphore_signal(barrier, inc=1, device_id=other, device_id_type=MESH)
            greeted += 1
        return greeted

    def ticket(self):
        self.used += 1
        return self.used - 1

    def copy(self, src, dst, ticket, device, link="core", hops=1):
        made = pltpu.make_async_remote_copy(
            src_ref=src, dst_ref=dst, send_sem=self.send.at[ticket],
            recv_sem=self.recv.at[ticket], device_id=device, device_id_type=MESH,
        )
        made.start()
        self.started.append(made)
        took = hops * math.prod(src.shape) * 2 / RATE[link]
        self.free[link] = max(self.free.get(link, 0.0), self.now) + took
        self.lands[ticket] = self.free[link] + HOP
        self.now += ISSUE

    def spawn(self, work):
        task = [work, None]
        self.tasks.append(task)
        self.step(task)
        return task

    def step(self, task):
        try:
            task[1] = next(task[0])
        except StopIteration:
            self.tasks.remove(task)

    def ready(self, task):
        wanted = task[1]
        if isinstance(wanted, list):
            return math.inf if any(other in self.tasks for other in wanted) else self.now
        return self.lands.get(wanted, math.inf)

    def run(self):
        while self.tasks:
            task = min(self.tasks, key=self.ready)
            self.now = max(self.now, self.ready(task)) + ISSUE
            self.step(task)

    def arrive(self, dst, ticket):
        pltpu.make_async_remote_copy(
            src_ref=dst, dst_ref=dst, send_sem=self.send.at[ticket],
            recv_sem=self.recv.at[ticket], device_id=self.sibling(), device_id_type=MESH,
        ).wait_recv()

    def finish(self):
        for made in self.started:
            made.wait_send()

    def reduce(self, buf, base, rows, axis, slots, spot):
        n = self.size[axis]
        if n == 1:
            return
        lanes = [(1, n // 2), (-1, n // 2 - 1)]
        subs = 2 if rows % 2 == 0 else 1
        per = rows // subs
        tickets, places = {}, {}
        for sub in range(subs):
            for lane, (_, steps) in enumerate(lanes):
                tickets[lane, sub] = [self.ticket() for _ in range(steps)]
                places[lane, sub] = [spot + per * k for k in range(steps)]
                spot += per * steps

        def own(shift, sub):
            return pl.ds(base + self.place(axis, shift) * rows + sub * per, per)

        def chain(lane, sub, way, steps):
            ticket, spots = tickets[lane, sub], places[lane, sub]
            for t in range(steps):
                mine = own(-way * self.turn * (steps - t), sub)
                if t == 0:
                    source = buf.at[mine]
                else:
                    source = slots.at[pl.ds(spots[t - 1], per)]
                    yield ticket[t - 1]
                    self.arrive(source, ticket[t - 1])
                    source[...] = (source[...].astype(F32) + buf[mine].astype(F32)).astype(BF16)
                self.copy(
                    source, slots.at[pl.ds(spots[t], per)], ticket[t],
                    self.device(axis, -way * self.turn), axis,
                )

        for sub in range(subs):
            for lane, (way, steps) in enumerate(lanes):
                if steps:
                    self.spawn(chain(lane, sub, way, steps))
        for sub in range(subs):
            total = buf[own(0, sub)].astype(F32)
            for lane, (way, steps) in enumerate(lanes):
                if steps:
                    source = slots.at[pl.ds(places[lane, sub][-1], per)]
                    yield tickets[lane, sub][-1]
                    self.arrive(source, tickets[lane, sub][-1])
                    total = total + source[...].astype(F32)
            buf[own(0, sub)] = total.astype(BF16)

    def far_first(self, axis):
        return sorted(range(1, self.size[axis]), key=lambda k: -min(k, self.size[axis] - k))

    def reduce_direct(self, buf, base, rows, axis, slots, spot):
        waits = []
        for k in self.far_first(axis):
            ticket = self.ticket()
            start = base + self.place(axis, k * self.turn) * rows
            slot = slots.at[pl.ds(spot + (k - 1) * rows, rows)]
            hops = min(k, self.size[axis] - k)
            self.copy(
                buf.at[pl.ds(start, rows)], slot, ticket,
                self.device(axis, k * self.turn), axis, hops,
            )
            waits.append((ticket, slot))
        here = pl.ds(base + self.at[axis] * rows, rows)
        total = buf[here].astype(F32)
        for ticket, slot in waits:
            yield ticket
            self.arrive(slot, ticket)
            total = total + slot[...].astype(F32)
        buf[here] = total.astype(BF16)

    def gather_direct(self, buf, base, rows, axis, arrived=None):
        def chunk(shift):
            start = base + self.place(axis, shift * self.turn) * rows
            return buf.at[pl.ds(start, rows)]

        waits = []
        for k in self.far_first(axis):
            ticket = self.ticket()
            hops = min(k, self.size[axis] - k)
            self.copy(
                chunk(0), chunk(0), ticket, self.device(axis, k * self.turn), axis, hops
            )
            waits.append((ticket, k))
        if arrived:
            arrived(0)
        for ticket, k in waits:
            yield ticket
            self.arrive(chunk(-k), ticket)
            if arrived:
                arrived(-k)

    def gather(self, buf, base, rows, axis, arrived=None):
        n = self.size[axis]
        if n == 1:
            if arrived:
                arrived(0)
            return
        lanes = [(1, n // 2), (-1, n // 2 - 1)]
        subs = 2 if rows % 2 == 0 else 1
        per = rows // subs
        tickets = {}
        for sub in range(subs):
            for lane, (_, steps) in enumerate(lanes):
                tickets[lane, sub] = [self.ticket() for _ in range(steps)]

        def chunk(shift, sub):
            return buf.at[pl.ds(base + self.place(axis, shift) * rows + sub * per, per)]

        def chain(lane, sub, way, steps):
            ticket = tickets[lane, sub]
            for t in range(steps + 1):
                block = chunk(way * self.turn * t, sub)
                if t > 0:
                    yield ticket[t - 1]
                    self.arrive(block, ticket[t - 1])
                if t < steps:
                    self.copy(block, block, ticket[t], self.device(axis, -way * self.turn), axis)
                if t > 0 and arrived:
                    arrived(way * t, sub, subs)

        chains = [
            self.spawn(chain(lane, sub, way, steps))
            for sub in range(subs)
            for lane, (way, steps) in enumerate(lanes)
            if steps
        ]
        if arrived:
            arrived(0)
        yield chains


def spread_out(rings, tab, base, total_rows, axes, forwards):
    mine = tab.at[rings.core]
    levels = []
    rows, start = total_rows, base
    for axis in axes:
        rows //= rings.size[axis]
        levels.append((axis, start, rows))
        start = start + rings.at[axis] * rows
    for depth in reversed(range(len(levels))):
        axis, first, rows = levels[depth]

        def forward(shift, sub=0, subs=1, axis=axis, first=first, rows=rows):
            ticket = rings.ticket()
            signed = shift * rings.turn
            per = rows // subs
            here = pl.ds(first + rings.place(axis, signed) * rows + sub * per, per)
            there = pl.ds(first + rings.place(axis, -signed) * rows + sub * per, per)
            rings.copy(tab.at[rings.core, here], tab.at[rings.core, here], ticket, rings.sibling())
            forwards.append((tab.at[1 - rings.core, there], ticket))

        step = rings.gather_direct if depth or axis in DIRECT else rings.gather
        yield from step(mine, first, rows, axis, forward if depth == 0 else None)


def collect(rings, buf, base, total_rows, axes, slots, spot):
    rows, start = total_rows, base
    for depth, axis in enumerate(axes):
        rows //= rings.size[axis]
        step = rings.reduce_direct if depth or axis in DIRECT else rings.reduce
        yield from step(buf, start, rows, axis, slots, spot)
        spot += rows * (rings.size[axis] - 1)
        start = start + rings.at[axis] * rows


def chunk_start(rings, base, total_rows, axes):
    rows, start = total_rows, base
    for axis in axes:
        rows //= rings.size[axis]
        start = start + rings.at[axis] * rows
    return start, rows


ATOM_ORDERS = (("y", "x", "z"), ("z", "y", "x"), ("x", "y", "z"))


def atoms_stage(rings, index_s, mom_ref, other, green_ref, tab_ref, pot_ref, dense, slots):
    nz, nx, ny = (rings.size[a] for a in "zxy")
    held = nz * nx * ny
    part_rows = held

    def place(slot, order):
        spots = {"z": slot // (nx * ny), "x": lax.rem(slot // ny, nx), "y": lax.rem(slot, ny)}
        index = 0
        for axis in order:
            index = index * rings.size[axis] + spots[axis]
        return index

    def fill(slot, carry):
        value = mom_ref[index_s[0, slot]] + other[index_s[1, slot]]
        for part, order in enumerate(ATOM_ORDERS):
            dense[part * part_rows + place(slot, order)] = value[part * HALF_S : (part + 1) * HALF_S]
        return carry

    lax.fori_loop(0, held, fill, 0, unroll=4)
    forwards = []
    green = green_ref[...]
    column = lax.broadcasted_iota(jnp.int32, (DEG, HALF_S, L), 2) // DEG
    layer = lax.broadcasted_iota(jnp.int32, (DEG, HALF_S, L), 0)

    def task(part):
        order = ATOM_ORDERS[part]
        base = part * part_rows
        yield from collect(rings, dense, base, part_rows, order, slots, base)
        start, rows = chunk_start(rings, base, part_rows, order)
        charges = dense[start].astype(F32)
        stacked = jnp.concatenate([charges[:, :L], charges[:, L:]], axis=0).astype(BF16)
        result = jnp.dot(green, stacked, preferred_element_type=F32)
        sides = []
        for par in range(2):
            block = result[par * DEG * HALF_S : (par + 1) * DEG * HALF_S].reshape(DEG, HALF_S, L)
            sides.append(jnp.sum(jnp.where(column == layer, block, 0.0), axis=0))
        tab_ref[rings.core, start] = jnp.concatenate(sides, axis=1).astype(BF16)
        yield from spread_out(rings, tab_ref, base, part_rows, order, forwards)

    for part in range(3):
        rings.spawn(task(part))
    rings.run()
    for slot in range(ny):
        for part, order in enumerate(ATOM_ORDERS):
            index = 0
            for axis in order:
                index = index * rings.size[axis] + (slot if axis == "y" else rings.at[axis])
            pot_ref[slot, part * HALF_S : (part + 1) * HALF_S, :] = tab_ref[
                rings.core, part * part_rows + index
            ]
    for block, ticket in forwards:
        rings.arrive(block, ticket)


def field_stage(
    atoms_s, blocks_s, w_ref, phi_ref, tab_ref, out_ref, dist_ref, polar_ref, side_ref,
    acc_ref, operand_ref, pad_ref, mid_ref, inv_ref,
):
    count = dist_ref.shape[0] * 8
    basis, points = phi_ref.shape
    piece = basis // 2
    held = tab_ref.shape[1] // 3
    nx, planes = lax.axis_size("batch_1"), lax.axis_size("row") * lax.axis_size("col")
    sizes = {"z": lax.axis_size("batch_0"), "x": nx, "y": planes}
    wide = mid_ref.shape[1]
    row = lax.broadcasted_iota(jnp.int32, (S, wide), 0)
    shell = jnp.where(row < HALF_S, 2 * row, 2 * (row - HALF_S) + 1)
    acc_ref[...] = jnp.zeros_like(acc_ref)

    def eight(group, carry):
        for u in range(8):
            k = group * 8 + u
            atom = atoms_s[0, k]
            live = shell < 8 * blocks_s[atom]
            spots = {
                "z": lax.div(atom, nx * 2 * planes),
                "x": lax.rem(lax.div(atom, 2 * planes), nx),
                "y": lax.rem(atom, planes),
            }
            packed = []
            for part, order in enumerate(ATOM_ORDERS):
                index = 0
                for axis in order:
                    index = index * sizes[axis] + spots[axis]
                packed.append(tab_ref[lax.rem(lax.div(atom, planes), 2), part * held + index])
            packed = jnp.concatenate(packed, axis=0)
            table = jnp.concatenate([packed[:, :L], packed[:, L:]], axis=0)
            for first in range(0, points, wide):
                cols = slice(first, first + wide)
                ang = angular_of(polar_ref, side_ref, group, u, cols)
                spread = jnp.dot(table, ang, preferred_element_type=F32)
                rad = radial_of(dist_ref[group, u : u + 1, cols], mid_ref[...], inv_ref[...], live)
                for c in range(3):
                    total = acc_ref[c, :, cols]
                    for par in range(2):
                        row = par * 96 + c * HALF_S
                        prod = spread[row : row + HALF_S] * rad[par * HALF_S : (par + 1) * HALF_S]
                        for g in range(0, HALF_S, 8):
                            total = total + prod[g : g + 8]
                    acc_ref[c, :, cols] = total
        return carry

    lax.fori_loop(0, count // 8, eight, 0)
    for q in range(2):
        pad_ref[q, :piece, :] = phi_ref[q * piece : (q + 1) * piece, :]
        pad_ref[q, piece:, :] = jnp.zeros((128 - piece, points), BF16)
    for c in range(3):
        field = jnp.sum(acc_ref[c], axis=0, keepdims=True) * w_ref[...]
        for first in range(0, points, wide):
            cols = slice(first, first + wide)
            operand_ref[:, cols] = (phi_ref[:, cols].astype(F32) * field[:, cols]).astype(BF16)
        for q in range(2):
            local = lax.dot_general(
                operand_ref[...], pad_ref[q], NT, preferred_element_type=F32
            ).astype(BF16)
            for r in range(2):
                out_ref[r * 2 + q, c] = local[r * piece : (r + 1) * piece]


TILE_ORDERS = (("z", "x"), ("x", "z"))


def square_peers():
    n_row, n_col = lax.axis_size("row"), lax.axis_size("col")
    return [
        {
            "batch_2": lax.rem(lax.axis_index("batch_2") + dc, 2),
            "row": lax.rem(lax.axis_index("row") + dr, n_row),
            "col": lax.rem(lax.axis_index("col") + dl, n_col),
        }
        for dc in range(2)
        for dr in range(n_row)
        for dl in range(n_col)
        if dc or dr or dl
    ]


def matrix_stage(
    rings, labels, quads_ref, label_ref, out_ref, tab_ref, flat, slots, got, marks, placed, hit
):
    row, col, core = (lax.axis_index(a) for a in ("row", "col", "batch_2"))
    n_row, n_col = lax.axis_size("row"), lax.axis_size("col")
    piece = quads_ref.shape[2]
    tile = hit.shape[0]
    half = tile // 2
    waits = []
    for j, to in enumerate(square_peers()):
        waits.append((got.at[j + 1], rings.ticket()))
        wanted = quads_ref.at[to["row"] * 2 + to["col"], pl.ds(to["batch_2"], 2)]
        rings.copy(wanted, *waits[j], to)
    marks[0] = label_ref[...]
    got[0] = quads_ref[row * 2 + col, pl.ds(core, 2)]
    padded = flat.shape[0] - 3 * half * (tile // 128) // 16
    flat[flat.shape[0] - padded :] = jnp.zeros((padded, 16, 128), BF16)
    for mark, ticket in labels:
        rings.arrive(mark, ticket)
    sources = 2 * n_row * n_col
    for s in range(sources):
        label = marks[s]
        cols_at = jnp.where(col == 0, label[0:1, :], label[1:2, :]) - col * tile
        col_hit = lax.broadcasted_iota(jnp.int32, (tile, 128), 0) == cols_at
        hit[:, s * 128 : (s + 1) * 128] = jnp.where(col_hit, 1.0, 0.0).astype(BF16)
    near = [0] + sorted(range(1, sources), key=lambda s: (s % (n_row * n_col) != 0, s % 4 == 1))
    for s in near:
        if s:
            rings.arrive(*waits[s - 1])
        label = marks[s]
        rows_at = jnp.where(row == 0, label[0:1, :], label[1:2, :]) - row * tile
        for first, count, shift, which in ((0, tile, 0, core), (tile, half, core * half, 1 - core)):
            row_hit = lax.broadcasted_iota(jnp.int32, (count, 128), 0) == rows_at - shift
            row_hit = jnp.where(row_hit, 1.0, 0.0).astype(BF16)[:, :piece]
            spread = jnp.dot(row_hit, got[s, which], preferred_element_type=F32).astype(BF16)
            placed[first : first + count, s * 128 : (s + 1) * 128] = spread
    groups = tile // 128
    for c in range(3):
        for j in range(tile // 256):
            block = lax.dot_general(
                placed[c * half : (c + 1) * half, :], hit[j * 256 : (j + 1) * 256, :], NT,
                preferred_element_type=F32,
            ).astype(BF16)
            for h in range(2):
                start = (c * groups + 2 * j + h) * half // 16
                flat[start : start + half // 16] = block[:, h * 128 : (h + 1) * 128].reshape(
                    half // 16, 16, 128
                )
    part_rows = flat.shape[0] // 2
    forwards = []

    def task(part):
        order = TILE_ORDERS[part]
        base = part * part_rows
        yield from collect(rings, flat, base, part_rows, order, slots, base)
        start, rows = chunk_start(rings, base, part_rows, order)
        here = pl.ds(start, rows)
        tab_ref[rings.core, here] = flat[here]
        yield from spread_out(rings, tab_ref, base, part_rows, order, forwards)

    for part in range(2):
        rings.spawn(task(part))
    rings.run()
    for block, ticket in forwards:
        rings.arrive(block, ticket)
    for h in range(2):
        for c, (comp, first) in enumerate(((2 * h, 0), (2 * h, half), (1, h * half))):
            for g in range(groups):
                start = (c * groups + g) * half // 16
                out_ref[comp, first : first + half, g * 128 : (g + 1) * 128] = tab_ref[
                    h, start : start + half // 16
                ].reshape(half, 128)


def whole_kernel(
    index_s, atoms_s, blocks_s, atoms_ref, pos_ref, pts_ref, w_ref, widths_ref, phi_ref, dens_ref,
    green_ref, basis_ref, pot_ref, out_ref,
    dist, polar, side, wd, scaled, ang, mid, inv, mom, other,
    dense, slots, tab, acc, operand, pad, quads, flat, slots_2, tab_2, got, marks, placed, hit,
    label, stage_a, stage_b, send, recv,
):
    rings = Rings(send, recv)
    met = [peer for peer in square_peers()]
    greeted = rings.greet("zx", met)
    none = jnp.full((8, 128), -(1 << 20), jnp.int32)
    label[...] = none
    piece = basis_ref.shape[1] // 2
    for q in range(2):
        part = basis_ref[:, q * piece : (q + 1) * piece]
        label[q : q + 1, :] = jnp.concatenate([part, none[:1, piece:]], axis=1)
    early = stage_a.shape[0]
    labels, halves = [], []

    def send_early():
        pl.semaphore_wait(pltpu.get_barrier_semaphore(), greeted)
        stage_a[...] = mom[:early]
        halves.append((other.at[pl.ds(0, early)], rings.ticket()))
        rings.copy(stage_a, *halves[0], rings.sibling())
        for j, to in enumerate(met):
            labels.append((marks.at[j + 1], rings.ticket()))
            rings.copy(label, *labels[j], to)

    moments_stage(
        atoms_s, blocks_s, atoms_ref, pos_ref, pts_ref, w_ref, widths_ref, phi_ref, dens_ref,
        mom, dist, polar, side, wd, scaled, ang, mid, inv, send_early,
    )
    stage_b[...] = mom[early:]
    halves.append((other.at[pl.ds(early, stage_b.shape[0])], rings.ticket()))
    rings.copy(stage_b, *halves[1], rings.sibling())
    for block, ticket in halves:
        rings.arrive(block, ticket)
    atoms_stage(rings, index_s, mom, other, green_ref, tab, pot_ref, dense, slots)
    field_stage(
        atoms_s, blocks_s, w_ref, phi_ref, tab, quads, dist, polar, side, acc, operand, pad, mid, inv
    )
    matrix_stage(
        rings, labels, quads, label, out_ref, tab_2, flat, slots_2, got, marks, placed, hit
    )
    rings.finish()


def whole_call(index, atoms, blocks, pos, pts, w, widths, phi, dens, green, labels, sizes):
    count = atoms.shape[1]
    basis, points = phi.shape
    ring_devices, planes, tile = sizes
    held = ring_devices * planes
    half = tile // 2
    unit = 2 * 16 * ring_devices
    rows = -(-(3 * half * (tile // 128)) // unit) * unit
    sources = 2 * planes
    wide = min(256, points)
    return pl.pallas_call(
        whole_kernel,
        out_shape=(
            jax.ShapeDtypeStruct((planes, 96, 128), BF16),
            jax.ShapeDtypeStruct((3, tile, tile), BF16),
        ),
        in_specs=[smem()] * 3 + [vmem()] * 9,
        out_specs=(vmem(), vmem()),
        scratch_shapes=[
            pltpu.VMEM((count // 8, 8, points), F32),
            pltpu.VMEM((DEG, count // 8, 8, points), F32),
            pltpu.VMEM((DEG, count // 8, 8, points), F32),
            pltpu.VMEM((8, points), F32),
            pltpu.VMEM((2, 192, points), BF16),
            pltpu.VMEM((2, L, points), BF16),
            pltpu.VMEM((S, wide), F32),
            pltpu.VMEM((S, wide), F32),
            pltpu.VMEM((count + 1, 96, 128), BF16),
            pltpu.VMEM((count + 1, 96, 128), BF16),
            pltpu.VMEM((3 * held, HALF_S, 128), BF16),
            pltpu.VMEM((3 * held, HALF_S, 128), BF16),
            pltpu.VMEM((2, 3 * held, HALF_S, 128), BF16),
            pltpu.VMEM((3, 8, points), F32),
            pltpu.VMEM((basis, points), BF16),
            pltpu.VMEM((2, 128, points), BF16),
            pltpu.VMEM((4, 3, basis // 2, 128), BF16),
            pltpu.VMEM((rows // 16, 16, 128), BF16),
            pltpu.VMEM((rows // 16, 16, 128), BF16),
            pltpu.VMEM((2, rows // 16, 16, 128), BF16),
            pltpu.VMEM((sources, 2, basis // 2, 128), BF16),
            pltpu.VMEM((sources, 8, 128), jnp.int32),
            pltpu.VMEM((3 * half, sources * 128), BF16),
            pltpu.VMEM((tile, sources * 128), BF16),
            pltpu.VMEM((8, 128), jnp.int32),
            pltpu.VMEM((count // 2, 96, 128), BF16),
            pltpu.VMEM((count // 2 + 1, 96, 128), BF16),
            pltpu.SemaphoreType.DMA((256,)),
            pltpu.SemaphoreType.DMA((256,)),
        ],
        compiler_params=pltpu.CompilerParams(
            vmem_limit_bytes=VMEM_LIMIT, collective_id=0, has_side_effects=True
        ),
        name="whole",
    )(index, atoms, blocks, atoms, pos, pts, w, widths, phi, dens, green, labels)


def on_device(
    basis_values,
    density_matrix,
    points,
    weights,
    intersection,
    basis_index,
    atom_positions,
    shell_blocks,
    shell_widths,
    green,
):
    phi, dens, pts = basis_values[0], density_matrix[0], points.transpose(1, 0, 2)
    nz, nx = lax.axis_size("batch_0"), lax.axis_size("batch_1")
    n_row, n_col = lax.axis_size("row"), lax.axis_size("col")
    planes = n_row * n_col
    plane = lax.axis_index("col") * n_row + lax.axis_index("row")
    widths = shell_widths.reshape(1, S)

    count = intersection.shape[1]
    held = nz * nx * planes
    sibling_atoms = lax.ppermute(intersection, "batch_2", [(0, 1), (1, 0)])
    both = jnp.concatenate([intersection, sibling_atoms], axis=0)
    slot = jnp.arange(held)
    slot_atom = (slot // planes * 2 + lax.axis_index("batch_2")) * planes + slot % planes
    match = both[:, :, None] == slot_atom[None, None, :]
    index = count + jnp.sum(
        jnp.where(match, jnp.arange(count)[None, :, None] - count, 0), axis=1
    )
    mine = lax.dynamic_slice_in_dim(green, plane, 1, 0).reshape(DEG, HALF_S, 2, HALF_S, 2)
    mine = mine.transpose(2, 0, 1, 4, 3).reshape(2 * DEG * HALF_S, S)
    tile = NB // n_row
    potential, matrix = whole_call(
        index, intersection, shell_blocks, atom_positions, pts, weights, widths, phi, dens, mine, basis_index,
        (nz * nx, planes, tile),
    )
    return potential.reshape(planes, -1), matrix


def solution(mesh):
    split = (8, 4, 2) if mesh.shape["batch"] == 64 else (mesh.shape["batch"] // 4, 2, 2)
    finer = Mesh(
        mesh.devices.reshape(*split, mesh.shape["row"], mesh.shape["col"]),
        BATCH_ROW_COL,
    )
    placed = (
        P(BATCH_ROW_COL, None, None),
        P(BATCH_ROW_COL, None, None, None),
        P(BATCH_ROW_COL, None, None),
        P(BATCH_ROW_COL, None),
        P(BATCH_ROW_COL, None),
        P(BATCH_ROW_COL, None),
        P(),
        P(),
        P(),
        P(BATCH, None, None),
    )
    return jax.shard_map(
        on_device,
        mesh=finer,
        in_specs=placed,
        out_specs=(P(BATCH, None), P(None, "row", "col")),
        check_vma=False,
    )
```
